256 devices in a mesh: row: 16 (over z, core), col: 16 (over y, x).
Axes of the slice: x: 4, y: 4, z: 8, core: 2. Of those that a mesh axis runs over, the one named last changes fastest.
Arguments:
- gen_points: bfloat16 [8192, 512], P(('row', 'col')), may hold values from -8 to 8
- data_points: bfloat16 [16384, 512], P('col', 'row'), may hold values from -8 to 8
- data_potential: float32 [16384], P('col'), may hold values from -3 to 3
Outputs:
- gen_potential: float32 [8192], P('row')
- data_potential_out: float32 [16384], P('col')
- transport_target: float32 [512, 8192], P('col', 'row')
The draws below stay inside these ranges and needn't reach their ends.
All inputs are finite; a program needn't handle non-finite values.
Results may differ from the reference program's by a relative error of at most 0.0003.
Values may be sent and summed in bfloat16 or wider, within the bound.
No kernel may reach another device: no remote copies, remote signals or barrier semaphores. Data moves between devices by JAX's collectives and lax.ppermute only.
A program may use at most 64 MiB of HBM per device.

```python
import math
import jax
import jax.numpy as jnp
from jax import lax

F = 512
ITERS = 2
NGEN = 8192
NDATA = 16384


def draw_data_points(key, part):
    key = jax.random.fold_in(key, 2)
    return jax.random.truncated_normal(key, -6.0, 6.0, (NDATA, F), jnp.float32).astype(jnp.bfloat16)


def draw_gen_points(key, part):
    key = jax.random.fold_in(key, 1)
    return jax.random.truncated_normal(key, -6.0, 6.0, (NGEN, F), jnp.float32).astype(jnp.bfloat16)


def block_levels(key, extent, cuts, smallest, high):
    def one(dim, parts):
        draws = jax.random.uniform(jax.random.fold_in(jax.random.fold_in(key, 6), dim), (parts,), jnp.float32, smallest / len(cuts), high / len(cuts))
        return jnp.repeat(jnp.exp(draws), extent[dim] // parts).reshape((-1,) + (1,) * (len(extent) - dim - 1))

    gain = one(*cuts[0])
    for cut in cuts[1:]:
        gain = gain * one(*cut)
    return gain


def centred(key, extent, spread, bound, cuts=(), held_as=jnp.bfloat16):
    drawn = spread * jax.random.normal(key, extent, jnp.float32)
    if cuts:
        drawn = drawn * block_levels(key, extent, cuts, -0.22, 0.18)
    return jnp.clip(drawn, -bound, bound).astype(held_as)


def setup_inputs(seed: int = 0) -> dict:
    arg_keys = jax.random.split(jax.random.key(seed), 4)
    gen_points = draw_gen_points(jax.random.fold_in(arg_keys[3], 71), 0)
    data_points = draw_data_points(jax.random.fold_in(arg_keys[3], 71), 0)
    data_potential = centred(arg_keys[2], (NDATA,), 0.5, 3.0, ((0, 16),), jnp.float32)
    return dict(gen_points=gen_points, data_points=data_points, data_potential=data_potential)


EPS = 0.05


def row_update(cost, potential, gen_count, data_count):
    block = math.gcd(gen_count, 1024)

    def one_block(tile):
        scores = (potential[None, :] - tile) / EPS
        largest = jnp.max(scores, axis=1)
        total = jnp.sum(jnp.exp(scores - largest[:, None]), axis=1)
        return largest, total

    largest, total = lax.map(one_block, cost.reshape(gen_count // block, block, data_count))
    largest = largest.reshape(gen_count)
    total = total.reshape(gen_count)
    return -EPS * (largest + jnp.log(total)) + EPS * math.log(data_count), largest, total


def col_update(cost, potential, gen_count, data_count):
    block = math.gcd(gen_count, 1024)

    def step(carry, pieces):
        largest, total = carry
        tile, pot_block = pieces
        scores = (pot_block[:, None] - tile) / EPS
        fresh = jnp.maximum(largest, jnp.max(scores, axis=0))
        total = total * jnp.exp(largest - fresh) + jnp.sum(jnp.exp(scores - fresh[None, :]), axis=0)
        return (fresh, total), None

    start = (jnp.full((data_count,), -jnp.inf, jnp.float32), jnp.zeros((data_count,), jnp.float32))
    (largest, total), _ = lax.scan(step, start, (cost.reshape(gen_count // block, block, data_count), potential.reshape(gen_count // block, block)))
    return -EPS * (largest + jnp.log(total)) + EPS * math.log(gen_count)


def reference(gen_points, data_points, data_potential):
    gen_count = gen_points.shape[0]
    data_count = data_points.shape[0]
    features = gen_points.shape[1]
    block = math.gcd(gen_count, 1024)
    data_f32 = data_points.astype(jnp.float32)
    data_sq = jnp.sum(data_f32 * data_f32, axis=1)

    def build(piece):
        piece_f32 = piece.astype(jnp.float32)
        gen_sq = jnp.sum(piece_f32 * piece_f32, axis=1)
        cross = jnp.dot(piece, data_points.T, preferred_element_type=jnp.float32)
        return (gen_sq[:, None] + data_sq[None, :] - 2.0 * cross) / features

    cost = lax.map(build, gen_points.reshape(gen_count // block, block, features)).reshape(gen_count, data_count)
    potential = data_potential
    for step in range(ITERS):
        gen_pot, _, _ = row_update(cost, potential, gen_count, data_count)
        potential = col_update(cost, gen_pot, gen_count, data_count)
    gen_pot, largest, total = row_update(cost, potential, gen_count, data_count)

    def target_block(pieces):
        tile, top, tot = pieces
        scores = (potential[None, :] - tile) / EPS
        weights = jnp.exp(scores - top[:, None]) / tot[:, None]
        return jnp.dot(weights, data_f32, precision=lax.Precision.HIGHEST, preferred_element_type=jnp.float32)

    target = lax.map(target_block, (cost.reshape(gen_count // block, block, data_count), largest.reshape(gen_count // block, block), total.reshape(gen_count // block, block)))
    target = target.reshape(gen_count, features).T
    return gen_pot, potential, target
```

```python
import math

import jax
import jax.numpy as jnp
from jax import lax
from jax.experimental import pallas as pl
from jax.experimental.pallas import tpu as pltpu
from jax.sharding import PartitionSpec as P

ITERS = 2
EPS = 0.05
LN2 = math.log(2.0)
SCALE = 1.0 / (EPS * LN2)
LANES = 128


def vmem():
    return pl.BlockSpec(memory_space=pltpu.VMEM)


def params():
    return pltpu.CompilerParams(vmem_limit_bytes=40 * 1024 * 1024)


def in_vmem(array):
    return pltpu.with_memory_space_constraint(array, pltpu.VMEM)


def kernel_call(body, out_shape, args, scratch=()):
    return pl.pallas_call(
        body,
        out_shape=out_shape,
        in_specs=[vmem() for _ in args],
        out_specs=jax.tree.map(lambda _: vmem(), out_shape),
        scratch_shapes=list(scratch),
        compiler_params=params(),
    )(*args)


def log_sum(parts):
    top = jnp.max(parts, axis=0)
    return top + jnp.log2(jnp.sum(jnp.exp2(parts - top[None]), axis=0))


def lanes_to_rows(chunk):
    return jnp.broadcast_to(chunk, (LANES, LANES)).T


def rows_to_lanes(column):
    return jnp.broadcast_to(column, (LANES, LANES)).T[0:1, :]


def row_lse_into(out_ref, affinity_ref, potential, gen_rows):
    for n in range(gen_rows // LANES):
        tile = affinity_ref[n * LANES : (n + 1) * LANES, :] + potential
        top = jnp.max(tile, axis=1, keepdims=True)
        total = jnp.sum(jnp.exp2(tile - top), axis=1, keepdims=True)
        line = rows_to_lanes(top + jnp.log2(total))
        out_ref[:, n : n + 1, :] = jnp.broadcast_to(line[None], (out_ref.shape[0], 1, LANES))


def chunks_to_line(chunks):
    return jnp.concatenate([chunks[n : n + 1, :] for n in range(chunks.shape[0])], axis=1)


def build_kernel(gen_ref, own_ref, other_ref, pot_ref, affinity_ref, out_ref):
    gen_rows, features = gen_ref.shape
    half = own_ref.shape[1]
    gen = gen_ref[...]
    gen_f32 = gen.astype(jnp.float32)
    gen_sq = jnp.sum(gen_f32 * gen_f32, axis=1, keepdims=True)
    for part, data_ref in enumerate((own_ref, other_ref)):
        data = data_ref[...]
        data_f32 = data.astype(jnp.float32)
        data_sq = jnp.sum(data_f32 * data_f32, axis=0, keepdims=True)
        cross = jnp.dot(gen, data, preferred_element_type=jnp.float32)
        affinity_ref[:, part * half : (part + 1) * half] = (2.0 * cross - (gen_sq + data_sq)) * (SCALE / features)
    potential = chunks_to_line(pot_ref[...])
    row_lse_into(out_ref, affinity_ref, potential, gen_rows)


def col_kernel(log_data, affinity_ref, got_ref, swap_ref, out_ref):
    gen_rows, data_cols = affinity_ref.shape
    row_log = log_sum(got_ref[...])
    top = jnp.full((8, data_cols), -jnp.inf, jnp.float32)
    for n in range(gen_rows // LANES):
        pot = log_data - lanes_to_rows(row_log[n : n + 1, :])
        pot = jnp.concatenate([pot] * (data_cols // LANES), axis=1)
        tile = affinity_ref[n * LANES : (n + 1) * LANES, :] + pot
        top = jnp.maximum(top, jnp.max(tile.reshape(LANES // 8, 8, data_cols), axis=0))
    top = jnp.max(top, axis=0, keepdims=True)
    total = jnp.zeros((8, data_cols), jnp.float32)
    for n in range(gen_rows // LANES):
        pot = log_data - lanes_to_rows(row_log[n : n + 1, :])
        pot = jnp.concatenate([pot] * (data_cols // LANES), axis=1)
        tile = affinity_ref[n * LANES : (n + 1) * LANES, :] + pot
        total = total + jnp.sum(jnp.exp2(tile - top).reshape(LANES // 8, 8, data_cols), axis=0)
    line = top + jnp.log2(jnp.sum(total, axis=0, keepdims=True))
    chunks = jnp.concatenate([line[:, n * LANES : (n + 1) * LANES] for n in range(data_cols // LANES)], axis=0)
    half = chunks.shape[0] // 2
    swapped = jnp.concatenate([chunks[half:], chunks[:half]], axis=0)
    chunks = jnp.where(swap_ref[...] > 0.0, swapped, chunks)
    out_ref[...] = jnp.broadcast_to(chunks[None], out_ref.shape)


def col_potential(got_ref, swap_ref, log_gen):
    chunks = log_gen - log_sum(got_ref[...])
    half = chunks.shape[0] // 2
    swapped = jnp.concatenate([chunks[half:], chunks[:half]], axis=0)
    return chunks, jnp.where(swap_ref[...] > 0.0, swapped, chunks)


def row_kernel(log_gen, affinity_ref, got_ref, swap_ref, out_ref):
    _, pot = col_potential(got_ref, swap_ref, log_gen)
    row_lse_into(out_ref, affinity_ref, chunks_to_line(pot), affinity_ref.shape[0])


def target_kernel(log_gen, affinity_ref, got_ref, swap_ref, own_ref, other_ref, pot_ref, out_ref, high, low):
    gen_rows, data_cols = affinity_ref.shape
    half = own_ref.shape[1]
    receivers = out_ref.shape[0]
    chunks = gen_rows // LANES
    feats = own_ref.shape[0] // receivers
    canonical, pot = col_potential(got_ref, swap_ref, log_gen)
    pot_ref[...] = canonical * (1.0 / SCALE)
    potential = chunks_to_line(pot)
    for n in range(chunks):
        rows = slice(n * LANES, (n + 1) * LANES)
        tile = affinity_ref[rows, :] + potential
        top = jnp.max(tile, axis=1, keepdims=True)
        weights = jnp.exp2(tile - top)
        total = jnp.sum(weights, axis=1, keepdims=True)
        upper = weights.astype(jnp.bfloat16)
        high[rows, :] = upper
        low[rows, :] = (weights - upper.astype(jnp.float32)).astype(jnp.bfloat16)
        base = chunks * feats
        for place, column in ((base + n, top), (base + chunks + n, total)):
            out_ref[:, place : place + 1, :] = jnp.broadcast_to(rows_to_lanes(column)[None], (receivers, 1, LANES))
    dims = (((1,), (1,)), ((), ()))
    for n in range(chunks):
        rows = slice(n * LANES, (n + 1) * LANES)
        sums = jnp.zeros((own_ref.shape[0], LANES), jnp.float32)
        for part, data_ref in enumerate((own_ref, other_ref)):
            cols = slice(part * half, (part + 1) * half)
            for piece in (high, low):
                sums = sums + lax.dot_general(data_ref[...], piece[rows, cols], dims, preferred_element_type=jnp.float32)
        out_ref[:, n * feats : (n + 1) * feats, :] = sums.reshape(receivers, feats, LANES)


def merge_kernel(log_data, got_ref, gen_pot_ref, target_ref):
    feats = target_ref.shape[0]
    chunks = target_ref.shape[1] // LANES
    base = chunks * feats
    tops = got_ref[:, base : base + chunks, :]
    totals = got_ref[:, base + chunks : base + 2 * chunks, :]
    top = jnp.max(tops, axis=0)
    factors = jnp.exp2(tops - top[None])
    total = jnp.sum(factors * totals, axis=0)
    gen_pot_ref[...] = (log_data - (top + jnp.log2(total))) * (1.0 / SCALE)
    factors = factors / total[None]
    for n in range(chunks):
        piece = got_ref[:, n * feats : (n + 1) * feats, :]
        target_ref[:, n * LANES : (n + 1) * LANES] = jnp.sum(piece * factors[:, n : n + 1, :], axis=0)


def local(gen_points, data_points, data_potential):
    f32 = jnp.float32
    rows_n, cols_n = lax.axis_size("row"), lax.axis_size("col")
    gen_rows = gen_points.shape[0] * cols_n
    data_cols = data_points.shape[0]
    features = gen_points.shape[1]
    log_data = math.log2(data_cols * cols_n)
    log_gen = math.log2(gen_rows * rows_n)
    half = data_cols // 2
    gen_chunks, data_chunks = gen_rows // LANES, data_cols // LANES

    core = lax.axis_index("row") % 2
    pieces = data_points.T.reshape(data_points.shape[1], 2, half).transpose(1, 0, 2)
    outgoing = jnp.broadcast_to(pieces[None], (rows_n // 2,) + pieces.shape).reshape((rows_n,) + pieces.shape[1:])
    own = lax.all_to_all(outgoing, "row", 0, 0).reshape(features, half)
    gen = lax.all_to_all(jnp.broadcast_to(gen_points[None], (cols_n,) + gen_points.shape), "col", 0, 0)
    gen = gen.reshape(gen_rows, features)
    other = lax.ppermute(own, "row", [(i, i ^ 1) for i in range(rows_n)])

    swap = jnp.broadcast_to(core.astype(f32), (data_chunks, LANES))
    start = (data_potential * SCALE).reshape(2, data_chunks // 2, LANES)
    start = jnp.where(core == 1, start[::-1], start).reshape(data_chunks, LANES)

    row_out = jax.ShapeDtypeStruct((cols_n, gen_chunks, LANES), f32)
    col_out = jax.ShapeDtypeStruct((rows_n, data_chunks, LANES), f32)

    def at(body, number):
        return lambda *refs: body(number, *refs)

    affinity, lines = kernel_call(
        build_kernel,
        (pltpu.VMEM((gen_rows, data_cols), f32), row_out),
        (gen, own, other, start),
    )
    affinity = in_vmem(affinity)
    for step in range(ITERS):
        got = lax.all_to_all(lines, "col", 0, 0)
        lines = kernel_call(at(col_kernel, log_data), col_out, (affinity, got, swap))
        got = lax.all_to_all(lines, "row", 0, 0)
        if step < ITERS - 1:
            lines = kernel_call(at(row_kernel, log_gen), row_out, (affinity, got, swap))
    feats = features // cols_n
    potential, lines = kernel_call(
        at(target_kernel, log_gen),
        (
            jax.ShapeDtypeStruct((data_chunks, LANES), f32),
            jax.ShapeDtypeStruct((cols_n, gen_chunks * (feats + 2), LANES), f32),
        ),
        (affinity, got, swap, own, other),
        scratch=[pltpu.VMEM((gen_rows, data_cols), jnp.bfloat16)] * 2,
    )
    got = lax.all_to_all(lines, "col", 0, 0)
    gen_pot, target = kernel_call(
        at(merge_kernel, log_data),
        (
            jax.ShapeDtypeStruct((gen_chunks, LANES), f32),
            jax.ShapeDtypeStruct((feats, gen_rows), f32),
        ),
        (got,),
    )
    return (gen_pot.reshape(gen_rows), potential.reshape(data_cols), target)


def solution(mesh):
    placed = (P(("row", "col"), None), P("col", "row"), P("col"))
    return jax.shard_map(
        local,
        mesh=mesh,
        in_specs=placed,
        out_specs=(P("row"), P("col"), P("col", "row")),
        check_vma=False,
    )
```

```python
import functools
import math

import jax
import jax.numpy as jnp
from jax import lax
from jax.experimental import pallas as pl
from jax.experimental.pallas import tpu as pltpu
from jax.sharding import PartitionSpec as P

ITERS = 2
EPS = 0.05
LN2 = math.log(2.0)
SCALE = 1.0 / (EPS * LN2)
LANES = 128


def in_vmem(array):
    return pltpu.with_memory_space_constraint(array, pltpu.VMEM)


def kernel_call(body, out_shape, args, scratch=(), scalars=0, flops=None, aliases=(), space=pltpu.VMEM):
    whole = pl.BlockSpec(memory_space=space)
    smem = pl.BlockSpec(memory_space=pltpu.SMEM)
    return pl.pallas_call(
        body,
        out_shape=out_shape,
        in_specs=[smem] * scalars + [whole] * (len(args) - scalars),
        out_specs=jax.tree.map(lambda _: whole, out_shape),
        scratch_shapes=list(scratch),
        input_output_aliases=dict(aliases),
        cost_estimate=flops and pl.CostEstimate(flops=flops, bytes_accessed=0, transcendentals=0),
        compiler_params=pltpu.CompilerParams(vmem_limit_bytes=16 * 1024 * 1024),
    )(*args)


def log_sum(parts):
    top = jnp.max(parts, axis=0)
    return top + jnp.log2(jnp.sum(jnp.exp2(parts - top[None]), axis=0))


def lanes_to_rows(chunk):
    return jnp.broadcast_to(chunk, (LANES, LANES)).T


def rows_to_lanes(column):
    return jnp.broadcast_to(column, (LANES, LANES)).T[0:1, :]


def chunks_to_line(chunks):
    return jnp.concatenate([chunks[n : n + 1, :] for n in range(chunks.shape[0])], axis=1)


def line_to_chunks(line):
    return jnp.concatenate([line[:, n : n + LANES] for n in range(0, line.shape[1], LANES)], axis=0)


def chunk(n):
    return slice(n * LANES, (n + 1) * LANES)


def halves(chunks):
    half = chunks.shape[0] // 2
    return [chunks_to_line(chunks[:half]), chunks_to_line(chunks[half:])]


def send_row_log_sums(refs, lines, out_ref):
    for n in range(refs[0].shape[0] // LANES):
        tiles = [ref[chunk(n), :] + line for ref, line in zip(refs, lines)]
        top = jnp.max(functools.reduce(jnp.maximum, tiles), axis=1, keepdims=True)
        total = jnp.sum(sum(jnp.exp2(tile - top) for tile in tiles), axis=1, keepdims=True)
        line = rows_to_lanes(top + jnp.log2(total))
        out_ref[:, n : n + 1, :] = jnp.broadcast_to(line[None], (out_ref.shape[0], 1, LANES))


def layout_kernel(data_ref, out_ref, sems):
    half = out_ref.shape[2]
    copies = [
        pltpu.make_async_copy(data_ref.at[:, pl.ds(n % 2 * half, half)], out_ref.at[n], sems.at[n])
        for n in range(out_ref.shape[0])
    ]
    for copy in copies:
        copy.start()
    for copy in copies:
        copy.wait()


def stack_kernel(*refs):
    for n, ref in enumerate(refs[:-1]):
        refs[-1][n, :, :] = ref[...]


def ordered_kernel(*_):
    pass


def affinity_of(gen, data):
    gen_f32, data_f32 = gen.astype(jnp.float32), data.astype(jnp.float32)
    gen_sq = jnp.sum(gen_f32 * gen_f32, axis=1, keepdims=True)
    data_sq = jnp.sum(data_f32 * data_f32, axis=0, keepdims=True)
    cross = jnp.dot(gen, data, preferred_element_type=jnp.float32)
    return (2.0 * cross - (gen_sq + data_sq)) * (SCALE / gen.shape[1])


def own_kernel(place_ref, g0, g1, g2, g3, data_ref, gen_ref, affinity_ref):
    rows = g0.shape[1]
    for a, ref in enumerate((g0, g1, g2, g3)):
        for b in range(ref.shape[0]):
            start = pl.multiple_of(place_ref[a * ref.shape[0] + b] * rows, rows)
            gen_ref[pl.ds(start, rows), :] = ref[b, :, :]
    affinity_ref[...] = affinity_of(gen_ref[...], data_ref[...])


def other_kernel(gen_ref, data_ref, own_ref, pot_ref, affinity_ref, out_ref):
    affinity_ref[...] = affinity_of(gen_ref[...], data_ref[...])
    send_row_log_sums([own_ref, affinity_ref], halves(pot_ref[...]), out_ref)


def swap_halves(chunks, swap_ref):
    half = chunks.shape[0] // 2
    swapped = jnp.concatenate([chunks[half:], chunks[:half]], axis=0)
    return jnp.where(swap_ref[...] > 0.0, swapped, chunks)


def col_kernel(log_data, own_ref, other_ref, got_ref, swap_ref, out_ref, pot_ref):
    gen_rows, half = own_ref.shape
    row_pot = log_data - log_sum(got_ref[...])
    for n in range(gen_rows // LANES):
        pot_ref[chunk(n), :] = lanes_to_rows(row_pot[n : n + 1, :])
    lines = []
    for ref in (own_ref, other_ref):

        def tile(n):
            return ref[chunk(n), :] + jnp.concatenate([pot_ref[chunk(n), :]] * (half // LANES), axis=1)

        def folded(values):
            return values.reshape(LANES // 8, 8, half)

        top = jnp.full((8, half), -jnp.inf, jnp.float32)
        for n in range(gen_rows // LANES):
            top = jnp.maximum(top, jnp.max(folded(tile(n)), axis=0))
        top = jnp.max(top, axis=0, keepdims=True)
        total = jnp.zeros((8, half), jnp.float32)
        for n in range(gen_rows // LANES):
            total = total + jnp.sum(folded(jnp.exp2(tile(n) - top)), axis=0)
        lines.append(line_to_chunks(top + jnp.log2(jnp.sum(total, axis=0, keepdims=True))))
    chunks = swap_halves(jnp.concatenate(lines, axis=0), swap_ref)
    out_ref[...] = jnp.broadcast_to(chunks[None], out_ref.shape)


def row_kernel(log_gen, own_ref, other_ref, got_ref, swap_ref, out_ref):
    pot = swap_halves(log_gen - log_sum(got_ref[...]), swap_ref)
    send_row_log_sums([own_ref, other_ref], halves(pot), out_ref)


def target_kernel(log_gen, own_ref, other_ref, got_ref, swap_ref, data_ref, more_ref, pot_ref, out_ref, high, low):
    gen_rows, half = own_ref.shape
    receivers = out_ref.shape[0]
    chunks = gen_rows // LANES
    features = data_ref.shape[0]
    feats = features // receivers
    base = chunks * feats
    pot = log_gen - log_sum(got_ref[...])
    pot_ref[...] = pot * (1.0 / SCALE)
    lines = halves(swap_halves(pot, swap_ref))
    dims = (((1,), (1,)), ((), ()))
    group = 2
    for first in range(0, chunks, group):
        for n in range(first, first + group):
            tiles = [ref[chunk(n), :] + line for ref, line in zip((own_ref, other_ref), lines)]
            top = jnp.max(jnp.maximum(*tiles), axis=1, keepdims=True)
            total = 0.0
            for part, tile in enumerate(tiles):
                weights = jnp.exp2(tile - top)
                total = total + weights
                upper = weights.astype(jnp.bfloat16)
                cols = slice(part * half, (part + 1) * half)
                high[chunk(n), cols] = upper
                low[chunk(n), cols] = (weights - upper.astype(jnp.float32)).astype(jnp.bfloat16)
            total = jnp.sum(total, axis=1, keepdims=True)
            for place, column in ((base + n, top), (base + chunks + n, total)):
                out_ref[:, place : place + 1, :] = jnp.broadcast_to(rows_to_lanes(column)[None], (receivers, 1, LANES))
        rows = slice(first * LANES, (first + group) * LANES)
        sums = jnp.zeros((features, group * LANES), jnp.float32)
        for part, ref in enumerate((data_ref, more_ref)):
            cols = slice(part * half, (part + 1) * half)
            for piece in (high, low):
                sums = sums + lax.dot_general(ref[...], piece[rows, cols], dims, preferred_element_type=jnp.float32)
        for n in range(group):
            out_ref[:, (first + n) * feats : (first + n + 1) * feats, :] = sums[:, chunk(n)].reshape(receivers, feats, LANES)


def merge_kernel(log_data, got_ref, gen_pot_ref, target_ref):
    feats = target_ref.shape[0]
    chunks = target_ref.shape[1] // LANES
    base = chunks * feats
    tops = got_ref[:, base : base + chunks, :]
    totals = got_ref[:, base + chunks : base + 2 * chunks, :]
    top = jnp.max(tops, axis=0)
    factors = jnp.exp2(tops - top[None])
    total = jnp.sum(factors * totals, axis=0)
    gen_pot_ref[...] = (log_data - (top + jnp.log2(total))) * (1.0 / SCALE)
    factors = factors / total[None]
    for n in range(chunks):
        piece = got_ref[:, n * feats : (n + 1) * feats, :]
        target_ref[:, chunk(n)] = jnp.sum(piece * factors[:, n : n + 1, :], axis=0)


def local(gen_points, data_points, data_potential):
    f32 = jnp.float32
    rows_n, cols_n = lax.axis_size("row"), lax.axis_size("col")
    gen_rows = gen_points.shape[0] * cols_n
    data_cols = data_points.shape[0]
    features = gen_points.shape[1]
    log_data = math.log2(data_cols * cols_n)
    log_gen = math.log2(gen_rows * rows_n)
    half = data_cols // 2
    gen_chunks, data_chunks = gen_rows // LANES, data_cols // LANES
    feats = features // cols_n
    dtype = gen_points.dtype
    shaped = jax.ShapeDtypeStruct

    side = math.isqrt(cols_n)
    offsets = (0, 1, side - 1, 2)

    def from_x(array, back):
        return lax.ppermute(array, "col", [(i, i - i % side + (i + back) % side) for i in range(cols_n)])

    def from_y(array, back):
        return lax.ppermute(array, "col", [(i, (i + back * side) % cols_n) for i in range(cols_n)])

    along_x = [from_x(gen_points, back) for back in offsets[1:]]
    outgoing = kernel_call(
        layout_kernel,
        shaped((rows_n, data_points.shape[1], half), dtype),
        (data_points.T,),
        scratch=[pltpu.SemaphoreType.DMA((rows_n,))],
        space=pl.ANY,
    )
    own = lax.all_to_all(outgoing, "row", 0, 0).reshape(features, half)
    stack = kernel_call(stack_kernel, shaped((side,) + gen_points.shape, dtype), (gen_points, *along_x))
    stacks = (stack,) + tuple(from_y(stack, back) for back in offsets[1:])

    core = lax.axis_index("row") % 2
    place = lax.axis_index("col")
    back = jnp.array(offsets, jnp.int32)
    places = (((place // side - back) % side)[:, None] * side + ((place % side - back) % side)[None, :]).reshape(-1)
    swap = jnp.broadcast_to(core.astype(f32), (data_chunks, LANES))
    start = (data_potential * SCALE).reshape(2, data_chunks // 2, LANES)
    start = jnp.where(core == 1, start[::-1], start).reshape(data_chunks, LANES)

    own = kernel_call(ordered_kernel, pltpu.VMEM(own.shape, dtype), (own, *stacks[1:]), aliases={0: 0})
    other = in_vmem(lax.ppermute(own, "row", [(i, i ^ 1) for i in range(rows_n)]))
    own = in_vmem(own)
    row_out = pltpu.VMEM((cols_n, gen_chunks, LANES), f32)
    col_out = pltpu.VMEM((rows_n, data_chunks, LANES), f32)
    block = pltpu.VMEM((gen_rows, half), f32)

    def at(body, number):
        return lambda *refs: body(number, *refs)

    gen, own_affinity = kernel_call(
        own_kernel,
        (pltpu.VMEM((gen_rows, features), dtype), block),
        (places, *stacks, own),
        scalars=1,
        flops=2 * gen_rows * half * features,
    )
    own_affinity = in_vmem(own_affinity)
    other_affinity, lines = kernel_call(other_kernel, (block, row_out), (gen, other, own_affinity, start))
    affinity = (own_affinity, in_vmem(other_affinity))
    for step in range(ITERS):
        got = lax.all_to_all(lines, "col", 0, 0)
        lines = kernel_call(
            at(col_kernel, log_data),
            col_out,
            (*affinity, got, swap),
            scratch=[pltpu.VMEM((gen_rows, LANES), f32)],
        )
        got = lax.all_to_all(lines, "row", 0, 0)
        if step < ITERS - 1:
            lines = kernel_call(at(row_kernel, log_gen), row_out, (*affinity, got, swap))
    potential, lines = kernel_call(
        at(target_kernel, log_gen),
        (shaped((data_chunks, LANES), f32), shaped((cols_n, gen_chunks * (feats + 2), LANES), f32)),
        (*affinity, got, swap, own, other),
        scratch=[pltpu.VMEM((gen_rows, data_cols), dtype)] * 2,
    )
    got = lax.all_to_all(lines, "col", 0, 0)
    gen_pot, target = kernel_call(
        at(merge_kernel, log_data),
        (shaped((gen_chunks, LANES), f32), shaped((feats, gen_rows), f32)),
        (got,),
    )
    return (gen_pot.reshape(gen_rows), potential.reshape(data_cols), target)


def solution(mesh):
    placed = (P(("row", "col"), None), P("col", "row"), P("col"))
    return jax.shard_map(
        local,
        mesh=mesh,
        in_specs=placed,
        out_specs=(P("row"), P("col"), P("col", "row")),
        check_vma=False,
    )
```

```python
import functools
import math

import jax
import jax.numpy as jnp
from jax import lax
from jax.experimental import pallas as pl
from jax.experimental.pallas import tpu as pltpu
from jax.sharding import PartitionSpec as P

ITERS = 2
EPS = 0.05
LN2 = math.log(2.0)
SCALE = 1.0 / (EPS * LN2)
LANES = 128
OFFSETS = (0, 1, -1, 2)


def in_vmem(array):
    return pltpu.with_memory_space_constraint(array, pltpu.VMEM)


def kernel_call(body, out_shape, args, scratch=(), flops=None, aliases=(), space=pltpu.VMEM):
    whole = pl.BlockSpec(memory_space=space)
    return pl.pallas_call(
        body,
        out_shape=out_shape,
        in_specs=[whole] * len(args),
        out_specs=jax.tree.map(lambda _: whole, out_shape),
        scratch_shapes=list(scratch),
        input_output_aliases=dict(aliases),
        cost_estimate=flops and pl.CostEstimate(flops=flops, bytes_accessed=0, transcendentals=0),
        compiler_params=pltpu.CompilerParams(vmem_limit_bytes=16 * 1024 * 1024),
    )(*args)


def log_sum(parts):
    top = jnp.max(parts, axis=0)
    return top + jnp.log2(jnp.sum(jnp.exp2(parts - top[None]), axis=0))


def lanes_to_rows(chunk):
    return jnp.broadcast_to(chunk, (LANES, LANES)).T


def rows_to_lanes(column):
    return jnp.broadcast_to(column, (LANES, LANES)).T[0:1, :]


def chunks_to_line(chunks):
    return jnp.concatenate([chunks[n : n + 1, :] for n in range(chunks.shape[0])], axis=1)


def line_to_chunks(line):
    return jnp.concatenate([line[:, n : n + LANES] for n in range(0, line.shape[1], LANES)], axis=0)


def chunk(n):
    return slice(n * LANES, (n + 1) * LANES)


def halves(chunks):
    half = chunks.shape[0] // 2
    return [chunks_to_line(chunks[:half]), chunks_to_line(chunks[half:])]


def send_row_log_sums(refs, lines, out_ref):
    for n in range(refs[0].shape[0] // LANES):
        tiles = [ref[chunk(n), :] + line for ref, line in zip(refs, lines)]
        top = jnp.max(functools.reduce(jnp.maximum, tiles), axis=1, keepdims=True)
        total = jnp.sum(sum(jnp.exp2(tile - top) for tile in tiles), axis=1, keepdims=True)
        line = rows_to_lanes(top + jnp.log2(total))
        out_ref[:, n : n + 1, :] = jnp.broadcast_to(line[None], (out_ref.shape[0], 1, LANES))


def layout_kernel(data_ref, out_ref, held, sems):
    half = out_ref.shape[2]
    arrivals = [
        pltpu.make_async_copy(data_ref.at[:, pl.ds(part * half, half)], held.at[part], sems.at[part]) for part in range(2)
    ]
    copies = [pltpu.make_async_copy(held.at[n % 2], out_ref.at[n], sems.at[2 + n]) for n in range(out_ref.shape[0])]
    for arrival in arrivals:
        arrival.start()
    for part, arrival in enumerate(arrivals):
        arrival.wait()
        for copy in copies[part::2]:
            copy.start()
    for copy in copies:
        copy.wait()


def stack_kernel(*refs):
    for n, ref in enumerate(refs[:-1]):
        refs[-1][n, :, :] = ref[...]


def ordered_kernel(*_):
    pass


def affinity_chunks(gen_ref, data_ref):
    data = data_ref[...]
    data_f32 = data.astype(jnp.float32)
    data_sq = jnp.sum(data_f32 * data_f32, axis=0, keepdims=True)
    for n in range(gen_ref.shape[0] // LANES):
        gen = gen_ref[chunk(n), :]
        gen_f32 = gen.astype(jnp.float32)
        gen_sq = jnp.sum(gen_f32 * gen_f32, axis=1, keepdims=True)
        cross = jnp.dot(gen, data, preferred_element_type=jnp.float32)
        yield chunk(n), (2.0 * cross - (gen_sq + data_sq)) * (SCALE / gen.shape[1])


def own_kernel(g0, g1, g2, g3, data_ref, gen_ref, affinity_ref):
    side, size = g0.shape[:2]
    column, core = lax.axis_index("col"), lax.axis_index("row") % 2
    for second, ref in zip(OFFSETS, (g0, g1, g2, g3)):
        for n, first in enumerate(OFFSETS):
            y_back = jnp.where(core == 0, second, first)
            x_back = jnp.where(core == 0, first, second)
            place = (column // side - y_back + side) % side * side + (column % side - x_back + side) % side
            gen_ref[pl.ds(pl.multiple_of(place * size, size), size), :] = ref[n, :, :]
    for rows, tile in affinity_chunks(gen_ref, data_ref):
        affinity_ref[rows, :] = tile


def other_kernel(gen_ref, data_ref, affinity_ref):
    for rows, tile in affinity_chunks(gen_ref, data_ref):
        affinity_ref[rows, :] = tile


def first_kernel(own_ref, other_ref, pot_ref, out_ref):
    send_row_log_sums((own_ref, other_ref), halves(swap_halves(pot_ref[...] * SCALE)), out_ref)


def swap_halves(chunks):
    half = chunks.shape[0] // 2
    swapped = jnp.concatenate([chunks[half:], chunks[:half]], axis=0)
    return jnp.where(lax.axis_index("row") % 2 == 1, swapped, chunks)


def col_kernel(log_data, own_ref, other_ref, got_ref, out_ref, pot_ref):
    gen_rows, half = own_ref.shape
    row_pot = log_data - log_sum(got_ref[...])
    for n in range(gen_rows // LANES):
        pot_ref[chunk(n), :] = lanes_to_rows(row_pot[n : n + 1, :])
    lines = []
    for ref in (own_ref, other_ref):

        def tile(n):
            return ref[chunk(n), :] + jnp.concatenate([pot_ref[chunk(n), :]] * (half // LANES), axis=1)

        def folded(values):
            return values.reshape(LANES // 8, 8, half)

        top = jnp.full((8, half), -jnp.inf, jnp.float32)
        for n in range(gen_rows // LANES):
            top = jnp.maximum(top, jnp.max(folded(tile(n)), axis=0))
        top = jnp.max(top, axis=0, keepdims=True)
        total = jnp.zeros((8, half), jnp.float32)
        for n in range(gen_rows // LANES):
            total = total + jnp.sum(folded(jnp.exp2(tile(n) - top)), axis=0)
        lines.append(line_to_chunks(top + jnp.log2(jnp.sum(total, axis=0, keepdims=True))))
    chunks = swap_halves(jnp.concatenate(lines, axis=0))
    out_ref[...] = jnp.broadcast_to(chunks[None], out_ref.shape)


def row_kernel(log_gen, own_ref, other_ref, got_ref, out_ref):
    lines = halves(swap_halves(log_gen - log_sum(got_ref[...])))
    send_row_log_sums((own_ref, other_ref), lines, out_ref)


def target_kernel(log_gen, own_ref, other_ref, got_ref, data_ref, more_ref, pot_ref, out_ref, high, low):
    gen_rows, half = own_ref.shape
    receivers = out_ref.shape[0]
    chunks = gen_rows // LANES
    features = data_ref.shape[0]
    feats = features // receivers
    base = chunks * feats
    pot = log_gen - log_sum(got_ref[...])
    pot_ref[...] = pot * (1.0 / SCALE)
    lines = halves(swap_halves(pot))
    dims = (((1,), (1,)), ((), ()))
    group = 2
    for first in range(0, chunks, group):
        for n in range(first, first + group):
            tiles = [ref[chunk(n), :] + line for ref, line in zip((own_ref, other_ref), lines)]
            top = jnp.max(jnp.maximum(*tiles), axis=1, keepdims=True)
            total = 0.0
            for part, tile in enumerate(tiles):
                weights = jnp.exp2(tile - top)
                total = total + weights
                upper = weights.astype(jnp.bfloat16)
                cols = slice(part * half, (part + 1) * half)
                high[chunk(n), cols] = upper
                low[chunk(n), cols] = (weights - upper.astype(jnp.float32)).astype(jnp.bfloat16)
            total = jnp.sum(total, axis=1, keepdims=True)
            for place, column in ((base + n, top), (base + chunks + n, total)):
                out_ref[:, place : place + 1, :] = jnp.broadcast_to(rows_to_lanes(column)[None], (receivers, 1, LANES))
        rows = slice(first * LANES, (first + group) * LANES)
        sums = jnp.zeros((features, group * LANES), jnp.float32)
        for part, ref in enumerate((data_ref, more_ref)):
            cols = slice(part * half, (part + 1) * half)
            for piece in (high, low):
                sums = sums + lax.dot_general(ref[...], piece[rows, cols], dims, preferred_element_type=jnp.float32)
        for n in range(group):
            out_ref[:, (first + n) * feats : (first + n + 1) * feats, :] = sums[:, chunk(n)].reshape(receivers, feats, LANES)


def merge_kernel(log_data, got_ref, gen_pot_ref, target_ref):
    feats = target_ref.shape[0]
    chunks = target_ref.shape[1] // LANES
    base = chunks * feats
    tops = got_ref[:, base : base + chunks, :]
    totals = got_ref[:, base + chunks : base + 2 * chunks, :]
    top = jnp.max(tops, axis=0)
    factors = jnp.exp2(tops - top[None])
    total = jnp.sum(factors * totals, axis=0)
    gen_pot_ref[...] = (log_data - (top + jnp.log2(total))) * (1.0 / SCALE)
    factors = factors / total[None]
    for n in range(chunks):
        piece = got_ref[:, n * feats : (n + 1) * feats, :]
        target_ref[:, chunk(n)] = jnp.sum(piece * factors[:, n : n + 1, :], axis=0)


def local(gen_points, data_points, data_potential):
    f32 = jnp.float32
    rows_n, cols_n = lax.axis_size("row"), lax.axis_size("col")
    gen_rows = gen_points.shape[0] * cols_n
    data_cols = data_points.shape[0]
    features = gen_points.shape[1]
    log_data = math.log2(data_cols * cols_n)
    log_gen = math.log2(gen_rows * rows_n)
    half = data_cols // 2
    gen_chunks, data_chunks = gen_rows // LANES, data_cols // LANES
    feats = features // cols_n
    dtype = gen_points.dtype
    shaped = jax.ShapeDtypeStruct

    side = math.isqrt(cols_n)

    def hop(array, phase, back):
        pairs = []
        for row in range(rows_n):
            for y in range(side):
                for x in range(side):
                    along_y = (row + phase) % 2
                    to_y, to_x = (y + back * along_y) % side, (x + back * (1 - along_y)) % side
                    pairs.append(((row * side + y) * side + x, (row * side + to_y) * side + to_x))
        return lax.ppermute(array, ("row", "col"), pairs)

    feats_held = data_points.shape[1]
    outgoing = kernel_call(
        layout_kernel,
        shaped((rows_n, feats_held, half), dtype),
        (pltpu.with_memory_space_constraint(data_points.T, pltpu.HBM),),
        scratch=[pltpu.VMEM((2, feats_held, half), dtype), pltpu.SemaphoreType.DMA((2 + rows_n,))],
        space=pltpu.HBM,
    )
    own = lax.all_to_all(outgoing, "row", 0, 0).reshape(features, half)
    stack = kernel_call(stack_kernel, shaped((side,) + gen_points.shape, dtype), (gen_points, *(hop(gen_points, 0, back) for back in OFFSETS[1:])))
    stacks = (stack,) + tuple(hop(stack, 1, back) for back in OFFSETS[1:])

    start = data_potential.reshape(data_chunks, LANES)

    own = kernel_call(ordered_kernel, pltpu.VMEM(own.shape, dtype), (own, *stacks[1:]), aliases={0: 0})
    other = in_vmem(lax.ppermute(own, "row", [(i, i ^ 1) for i in range(rows_n)]))
    own = in_vmem(own)
    row_out = pltpu.VMEM((cols_n, gen_chunks, LANES), f32)
    col_out = pltpu.VMEM((rows_n, data_chunks, LANES), f32)
    block = pltpu.VMEM((gen_rows, half), f32)

    def at(body, number):
        return lambda *refs: body(number, *refs)

    gen, own_affinity = kernel_call(
        own_kernel,
        (pltpu.VMEM((gen_rows, features), dtype), block),
        (*stacks, own),
        flops=2 * gen_rows * half * features,
    )
    own_affinity = in_vmem(own_affinity)
    affinity = (own_affinity, in_vmem(kernel_call(other_kernel, block, (gen, other))))
    lines = kernel_call(first_kernel, row_out, (*affinity, start))
    for step in range(ITERS):
        got = lax.all_to_all(lines, "col", 0, 0)
        lines = kernel_call(
            at(col_kernel, log_data),
            col_out,
            (*affinity, got),
            scratch=[pltpu.VMEM((gen_rows, LANES), f32)],
        )
        got = lax.all_to_all(lines, "row", 0, 0)
        if step < ITERS - 1:
            lines = kernel_call(at(row_kernel, log_gen), row_out, (*affinity, got))
    potential, lines = kernel_call(
        at(target_kernel, log_gen),
        (shaped((data_chunks, LANES), f32), shaped((cols_n, gen_chunks * (feats + 2), LANES), f32)),
        (*affinity, got, own, other),
        scratch=[pltpu.VMEM((gen_rows, data_cols), dtype)] * 2,
    )
    got = lax.all_to_all(lines, "col", 0, 0)
    gen_pot, target = kernel_call(
        at(merge_kernel, log_data),
        (shaped((gen_chunks, LANES), f32), shaped((feats, gen_rows), f32)),
        (got,),
    )
    return (gen_pot.reshape(gen_rows), potential.reshape(data_cols), target)


def solution(mesh):
    placed = (P(("row", "col"), None), P("col", "row"), P("col"))
    return jax.shard_map(
        local,
        mesh=mesh,
        in_specs=placed,
        out_specs=(P("row"), P("col"), P("col", "row")),
        check_vma=False,
    )
```

```python
import functools
import math

import jax
import jax.numpy as jnp
from jax import lax
from jax.experimental import pallas as pl
from jax.experimental.pallas import tpu as pltpu
from jax.sharding import PartitionSpec as P

ITERS = 2
EPS = 0.05
LN2 = math.log(2.0)
SCALE = 1.0 / (EPS * LN2)
LANES = 128
OFFSETS = (0, 2, 1, -1)
STATS = 8


def in_vmem(array):
    return pltpu.with_memory_space_constraint(array, pltpu.VMEM)


def kernel_call(body, out_shape, args, scratch=(), flops=None, aliases=(), space=pltpu.VMEM):
    whole = pl.BlockSpec(memory_space=space)
    return pl.pallas_call(
        body,
        out_shape=out_shape,
        in_specs=[whole] * len(args),
        out_specs=jax.tree.map(lambda _: whole, out_shape),
        scratch_shapes=list(scratch),
        input_output_aliases=dict(aliases),
        cost_estimate=flops and pl.CostEstimate(flops=flops, bytes_accessed=0, transcendentals=0),
        compiler_params=pltpu.CompilerParams(vmem_limit_bytes=16 * 1024 * 1024),
    )(*args)


def log_sum(parts):
    top = jnp.max(parts, axis=0)
    return top + jnp.log2(jnp.sum(jnp.exp2(parts - top[None]), axis=0))


def lanes_to_rows(chunk):
    return jnp.broadcast_to(chunk, (LANES, LANES)).T


def rows_to_lanes(column):
    return jnp.broadcast_to(column, (LANES, LANES)).T[0:1, :]


def chunks_to_line(chunks):
    return jnp.concatenate([chunks[n : n + 1, :] for n in range(chunks.shape[0])], axis=1)


def line_to_chunks(line):
    return jnp.concatenate([line[:, n : n + LANES] for n in range(0, line.shape[1], LANES)], axis=0)


def chunk(n):
    return slice(n * LANES, (n + 1) * LANES)


def halves(chunks):
    half = chunks.shape[0] // 2
    return [chunks_to_line(chunks[:half]), chunks_to_line(chunks[half:])]


def send_row_log_sums(refs, lines, out_ref):
    for n in range(refs[0].shape[0] // LANES):
        tiles = [ref[chunk(n), :] + line for ref, line in zip(refs, lines)]
        top = jnp.max(functools.reduce(jnp.maximum, tiles), axis=1, keepdims=True)
        total = jnp.sum(sum(jnp.exp2(tile - top) for tile in tiles), axis=1, keepdims=True)
        line = rows_to_lanes(top + jnp.log2(total))
        out_ref[:, n : n + 1, :] = jnp.broadcast_to(line[None], (out_ref.shape[0], 1, LANES))


def layout_kernel(data_ref, out_ref, held, sems):
    half = out_ref.shape[2]
    arrivals = [
        pltpu.make_async_copy(data_ref.at[:, pl.ds(part * half, half)], held.at[part], sems.at[part]) for part in range(2)
    ]
    copies = [pltpu.make_async_copy(held.at[n % 2], out_ref.at[n], sems.at[2 + n]) for n in range(out_ref.shape[0])]
    for arrival in arrivals:
        arrival.start()
    for part, arrival in enumerate(arrivals):
        arrival.wait()
        for copy in copies[part::2]:
            copy.start()
    for copy in copies:
        copy.wait()


def stack_kernel(*refs):
    for n, ref in enumerate(refs[:-1]):
        refs[-1][n, :, :] = ref[...]


def ordered_kernel(*_):
    pass


def affinity_chunks(gen_ref, data_ref):
    data = data_ref[...]
    data_f32 = data.astype(jnp.float32)
    data_sq = jnp.sum(data_f32 * data_f32, axis=0, keepdims=True)
    for n in range(gen_ref.shape[0] // LANES):
        gen = gen_ref[chunk(n), :]
        gen_f32 = gen.astype(jnp.float32)
        gen_sq = jnp.sum(gen_f32 * gen_f32, axis=1, keepdims=True)
        cross = jnp.dot(gen, data, preferred_element_type=jnp.float32)
        yield chunk(n), (2.0 * cross - (gen_sq + data_sq)) * (SCALE / gen.shape[1])


def own_kernel(g0, g1, g2, g3, data_ref, gen_ref, affinity_ref):
    side, size = g0.shape[:2]
    column, core = lax.axis_index("col"), lax.axis_index("row") % 2
    for second, ref in zip(OFFSETS, (g0, g1, g2, g3)):
        for n, first in enumerate(OFFSETS):
            y_back = jnp.where(core == 0, second, first)
            x_back = jnp.where(core == 0, first, second)
            place = (column // side - y_back + side) % side * side + (column % side - x_back + side) % side
            gen_ref[pl.ds(pl.multiple_of(place * size, size), size), :] = ref[n, :, :]
    for rows, tile in affinity_chunks(gen_ref, data_ref):
        affinity_ref[rows, :] = tile


def other_kernel(gen_ref, data_ref, affinity_ref):
    for rows, tile in affinity_chunks(gen_ref, data_ref):
        affinity_ref[rows, :] = tile


def first_kernel(own_ref, other_ref, pot_ref, out_ref):
    send_row_log_sums((own_ref, other_ref), halves(swap_halves(pot_ref[...] * SCALE)), out_ref)


def swap_halves(chunks):
    half = chunks.shape[0] // 2
    swapped = jnp.concatenate([chunks[half:], chunks[:half]], axis=0)
    return jnp.where(lax.axis_index("row") % 2 == 1, swapped, chunks)


def col_kernel(log_data, own_ref, other_ref, got_ref, out_ref, pot_ref):
    gen_rows, half = own_ref.shape
    row_pot = log_data - log_sum(got_ref[...])
    for n in range(gen_rows // LANES):
        pot_ref[chunk(n), :] = lanes_to_rows(row_pot[n : n + 1, :])
    lines = []
    for ref in (own_ref, other_ref):

        def tile(n):
            return ref[chunk(n), :] + jnp.concatenate([pot_ref[chunk(n), :]] * (half // LANES), axis=1)

        def folded(values):
            return values.reshape(LANES // 8, 8, half)

        top = jnp.full((8, half), -jnp.inf, jnp.float32)
        for n in range(gen_rows // LANES):
            top = jnp.maximum(top, jnp.max(folded(tile(n)), axis=0))
        top = jnp.max(top, axis=0, keepdims=True)
        total = jnp.zeros((8, half), jnp.float32)
        for n in range(gen_rows // LANES):
            total = total + jnp.sum(folded(jnp.exp2(tile(n) - top)), axis=0)
        lines.append(line_to_chunks(top + jnp.log2(jnp.sum(total, axis=0, keepdims=True))))
    chunks = swap_halves(jnp.concatenate(lines, axis=0))
    out_ref[...] = jnp.broadcast_to(chunks[None], out_ref.shape)


def row_kernel(log_gen, own_ref, other_ref, got_ref, out_ref):
    lines = halves(swap_halves(log_gen - log_sum(got_ref[...])))
    send_row_log_sums((own_ref, other_ref), lines, out_ref)


def merged(refs):
    stats = jnp.stack([ref[ref.shape[0] - STATS :, :] for ref in refs])
    tops, totals = stats[:, : STATS // 2, :], stats[:, STATS // 2 :, :]
    top = jnp.max(tops, axis=0)
    factors = jnp.exp2(tops - top[None])
    return top, jnp.sum(factors * totals, axis=0), factors


def target_kernel(log_gen, own_ref, other_ref, got_ref, data_ref, more_ref, pot_ref, *refs):
    *outs, sums_ref, high, low = refs
    gen_rows, half = own_ref.shape
    chunks = gen_rows // LANES
    features = data_ref.shape[0]
    side = len(outs)
    feats = features // side**2
    pot = log_gen - log_sum(got_ref[...])
    pot_ref[...] = pot * (1.0 / SCALE)
    lines = halves(swap_halves(pot))
    dims = (((1,), (1,)), ((), ()))
    group = 2
    for first in range(0, chunks, group):
        for n in range(first, first + group):
            tiles = [ref[chunk(n), :] + line for ref, line in zip((own_ref, other_ref), lines)]
            top = jnp.max(jnp.maximum(*tiles), axis=1, keepdims=True)
            total = 0.0
            for part, tile in enumerate(tiles):
                weights = jnp.exp2(tile - top)
                total = total + weights
                upper = weights.astype(jnp.bfloat16)
                cols = slice(part * half, (part + 1) * half)
                high[chunk(n), cols] = upper
                low[chunk(n), cols] = (weights - upper.astype(jnp.float32)).astype(jnp.bfloat16)
            total = jnp.sum(total, axis=1, keepdims=True)
            for place, column in ((n, top), (chunks + n, total)):
                line = rows_to_lanes(column)
                for out_ref in outs:
                    out_ref[side * chunks * feats + place, :] = line[0]
        rows = slice(first * LANES, (first + group) * LANES)
        sums = jnp.zeros((features, group * LANES), jnp.float32)
        for part, ref in enumerate((data_ref, more_ref)):
            cols = slice(part * half, (part + 1) * half)
            for piece in (high, low):
                sums = sums + lax.dot_general(ref[...], piece[rows, cols], dims, preferred_element_type=jnp.float32)
        sums_ref[:, rows] = sums
    column, core = lax.axis_index("col"), lax.axis_index("row") % 2
    for offset, out_ref in zip(OFFSETS, outs):
        for second in range(side):
            y = jnp.where(core == 0, second, (column // side + offset + side) % side)
            x = jnp.where(core == 0, (column % side + offset + side) % side, second)
            source = pl.ds(pl.multiple_of((y * side + x) * feats, feats), feats)
            for n in range(chunks):
                place = (second * chunks + n) * feats
                out_ref[place : place + feats, :] = sums_ref[source, chunk(n)]


def relay_kernel(*refs):
    side = len(refs) // 2
    got, outs = refs[:side], refs[side:]
    top, total, factors = merged(got)
    chunks = top.shape[0]
    size = outs[0].shape[0] - STATS
    feats = size // chunks
    column, core = lax.axis_index("col"), lax.axis_index("row") % 2
    place = jnp.where(core == 0, column // side, column % side)
    for offset, out_ref in zip(OFFSETS, outs):
        start = (place + offset + side) % side * size
        for n in range(chunks):
            source = pl.ds(pl.multiple_of(start + n * feats, feats), feats)
            out_ref[n * feats : (n + 1) * feats, :] = sum(
                ref[source, :] * factors[sender, n : n + 1, :] for sender, ref in enumerate(got)
            )
        out_ref[size : size + chunks, :] = top
        out_ref[size + chunks :, :] = total


def merge_kernel(log_data, *refs):
    *got, gen_pot_ref, target_ref = refs
    top, total, factors = merged(got)
    feats = target_ref.shape[0]
    gen_pot_ref[...] = (log_data - (top + jnp.log2(total))) * (1.0 / SCALE)
    factors = factors / total[None]
    for n in range(top.shape[0]):
        target_ref[:, chunk(n)] = sum(
            ref[n * feats : (n + 1) * feats, :] * factors[sender, n : n + 1, :] for sender, ref in enumerate(got)
        )


def local(gen_points, data_points, data_potential):
    f32 = jnp.float32
    rows_n, cols_n = lax.axis_size("row"), lax.axis_size("col")
    gen_rows = gen_points.shape[0] * cols_n
    data_cols = data_points.shape[0]
    features = gen_points.shape[1]
    log_data = math.log2(data_cols * cols_n)
    log_gen = math.log2(gen_rows * rows_n)
    half = data_cols // 2
    gen_chunks, data_chunks = gen_rows // LANES, data_cols // LANES
    feats = features // cols_n
    dtype = gen_points.dtype
    shaped = jax.ShapeDtypeStruct

    side = math.isqrt(cols_n)

    def hop(array, phase, back):
        pairs = []
        for row in range(rows_n):
            for y in range(side):
                for x in range(side):
                    along_y = (row + phase) % 2
                    to_y, to_x = (y + back * along_y) % side, (x + back * (1 - along_y)) % side
                    pairs.append(((row * side + y) * side + x, (row * side + to_y) * side + to_x))
        return lax.ppermute(array, ("row", "col"), pairs)

    feats_held = data_points.shape[1]
    outgoing = kernel_call(
        layout_kernel,
        shaped((rows_n, feats_held, half), dtype),
        (pltpu.with_memory_space_constraint(data_points.T, pltpu.HBM),),
        scratch=[pltpu.VMEM((2, feats_held, half), dtype), pltpu.SemaphoreType.DMA((2 + rows_n,))],
        space=pltpu.HBM,
    )
    own = lax.all_to_all(outgoing, "row", 0, 0).reshape(features, half)
    stack = kernel_call(stack_kernel, shaped((side,) + gen_points.shape, dtype), (gen_points, *(hop(gen_points, 0, back) for back in OFFSETS[1:])))
    stacks = (stack,) + tuple(hop(stack, 1, back) for back in OFFSETS[1:])

    start = data_potential.reshape(data_chunks, LANES)

    own = kernel_call(ordered_kernel, pltpu.VMEM(own.shape, dtype), (own, *stacks[1:]), aliases={0: 0})
    other = in_vmem(lax.ppermute(own, "row", [(i, i ^ 1) for i in range(rows_n)]))
    own = in_vmem(own)
    row_out = pltpu.VMEM((cols_n, gen_chunks, LANES), f32)
    col_out = pltpu.VMEM((rows_n, data_chunks, LANES), f32)
    block = pltpu.VMEM((gen_rows, half), f32)

    def at(body, number):
        return lambda *refs: body(number, *refs)

    gen, own_affinity = kernel_call(
        own_kernel,
        (pltpu.VMEM((gen_rows, features), dtype), block),
        (*stacks, own),
        flops=2 * gen_rows * half * features,
    )
    own_affinity = in_vmem(own_affinity)
    affinity = (own_affinity, in_vmem(kernel_call(other_kernel, block, (gen, other))))
    lines = kernel_call(first_kernel, row_out, (*affinity, start))
    for step in range(ITERS):
        got = lax.all_to_all(lines, "col", 0, 0)
        lines = kernel_call(
            at(col_kernel, log_data),
            col_out,
            (*affinity, got),
            scratch=[pltpu.VMEM((gen_rows, LANES), f32)],
        )
        got = lax.all_to_all(lines, "row", 0, 0)
        if step < ITERS - 1:
            lines = kernel_call(at(row_kernel, log_gen), row_out, (*affinity, got))
    block_rows = gen_chunks * feats
    potential, *blocks = kernel_call(
        at(target_kernel, log_gen),
        (shaped((data_chunks, LANES), f32),) + (shaped((side * block_rows + STATS, LANES), f32),) * side,
        (*affinity, got, own, other),
        scratch=[pltpu.VMEM((features, gen_rows), f32)] + [pltpu.VMEM((gen_rows, data_cols), dtype)] * 2,
    )
    blocks = kernel_call(
        relay_kernel,
        (shaped((block_rows + STATS, LANES), f32),) * side,
        [blocks[0]] + [hop(block, 0, back) for block, back in zip(blocks[1:], OFFSETS[1:])],
    )
    gen_pot, target = kernel_call(
        at(merge_kernel, log_data),
        (shaped((gen_chunks, LANES), f32), shaped((feats, gen_rows), f32)),
        [blocks[0]] + [hop(block, 1, back) for block, back in zip(blocks[1:], OFFSETS[1:])],
    )
    return (gen_pot.reshape(gen_rows), potential.reshape(data_cols), target)


def solution(mesh):
    placed = (P(("row", "col"), None), P("col", "row"), P("col"))
    return jax.shard_map(
        local,
        mesh=mesh,
        in_specs=placed,
        out_specs=(P("row"), P("col"), P("col", "row")),
        check_vma=False,
    )
```

```python
import functools
import math

import jax
import jax.numpy as jnp
from jax import lax
from jax.experimental import pallas as pl
from jax.experimental.pallas import tpu as pltpu
from jax.sharding import PartitionSpec as P

ITERS = 2
EPS = 0.05
LN2 = math.log(2.0)
SCALE = 1.0 / (EPS * LN2)
LANES = 128
OFFSETS = (0, 2, 1, -1)
STATS = 8


def in_vmem(array):
    return pltpu.with_memory_space_constraint(array, pltpu.VMEM)


def kernel_call(body, out_shape, args, scratch=(), flops=None, aliases=(), space=pltpu.VMEM):
    whole = pl.BlockSpec(memory_space=space)
    return pl.pallas_call(
        body,
        out_shape=out_shape,
        in_specs=[whole] * len(args),
        out_specs=jax.tree.map(lambda _: whole, out_shape),
        scratch_shapes=list(scratch),
        input_output_aliases=dict(aliases),
        cost_estimate=flops and pl.CostEstimate(flops=flops, bytes_accessed=0, transcendentals=0),
        compiler_params=pltpu.CompilerParams(vmem_limit_bytes=16 * 1024 * 1024),
    )(*args)


def log_sum(parts):
    top = jnp.max(parts, axis=0)
    return top + jnp.log2(jnp.sum(jnp.exp2(parts - top[None]), axis=0))


def lanes_to_rows(chunk):
    return jnp.broadcast_to(chunk, (LANES, LANES)).T


def rows_to_lanes(column):
    return jnp.broadcast_to(column, (LANES, LANES)).T[0:1, :]


def chunks_to_line(chunks):
    return jnp.concatenate([chunks[n : n + 1, :] for n in range(chunks.shape[0])], axis=1)


def line_to_chunks(line):
    return jnp.concatenate([line[:, n : n + LANES] for n in range(0, line.shape[1], LANES)], axis=0)


def chunk(n):
    return slice(n * LANES, (n + 1) * LANES)


def halves(chunks):
    half = chunks.shape[0] // 2
    return [chunks_to_line(chunks[:half]), chunks_to_line(chunks[half:])]


def row_log_sums(tiles):
    top = jnp.max(functools.reduce(jnp.maximum, tiles), axis=1, keepdims=True)
    total = jnp.sum(sum(jnp.exp2(tile - top) for tile in tiles), axis=1, keepdims=True)
    return rows_to_lanes(top + jnp.log2(total))


def layout_kernel(data_ref, out_ref, held, sems):
    half = out_ref.shape[2]
    arrivals = [
        pltpu.make_async_copy(data_ref.at[:, pl.ds(part * half, half)], held.at[part], sems.at[part]) for part in range(2)
    ]
    copies = [pltpu.make_async_copy(held.at[n % 2], out_ref.at[n], sems.at[2 + n]) for n in range(out_ref.shape[0])]
    for arrival in arrivals:
        arrival.start()
    for part, arrival in enumerate(arrivals):
        arrival.wait()
        for copy in copies[part::2]:
            copy.start()
    for copy in copies:
        copy.wait()


def stack_kernel(*refs):
    for n, ref in enumerate(refs[:-1]):
        refs[-1][n, :, :] = ref[...]


def ordered_kernel(*_):
    pass


def affinity_chunks(gen_ref, data_ref):
    data = data_ref[...]
    data_f32 = data.astype(jnp.float32)
    data_sq = jnp.sum(data_f32 * data_f32, axis=0, keepdims=True)
    for n in range(gen_ref.shape[0] // LANES):
        gen = gen_ref[chunk(n), :]
        gen_f32 = gen.astype(jnp.float32)
        gen_sq = jnp.sum(gen_f32 * gen_f32, axis=1, keepdims=True)
        cross = jnp.dot(gen, data, preferred_element_type=jnp.float32)
        yield chunk(n), (2.0 * cross - (gen_sq + data_sq)) * (SCALE / gen.shape[1])


def own_kernel(g0, g1, g2, g3, data_ref, pot_ref, gen_ref, affinity_ref, log_ref):
    side, size = g0.shape[:2]
    column, core = lax.axis_index("col"), lax.axis_index("row") % 2
    for second, ref in zip(OFFSETS, (g0, g1, g2, g3)):
        for n, first in enumerate(OFFSETS):
            y_back = jnp.where(core == 0, second, first)
            x_back = jnp.where(core == 0, first, second)
            place = (column // side - y_back + side) % side * side + (column % side - x_back + side) % side
            gen_ref[pl.ds(pl.multiple_of(place * size, size), size), :] = ref[n, :, :]
    line = halves(swap_halves(pot_ref[...] * SCALE))[0]
    for n, (rows, tile) in enumerate(affinity_chunks(gen_ref, data_ref)):
        affinity_ref[rows, :] = tile
        log_ref[n : n + 1, :] = row_log_sums([tile + line])


def other_kernel(gen_ref, data_ref, affinity_ref):
    for rows, tile in affinity_chunks(gen_ref, data_ref):
        affinity_ref[rows, :] = tile


def first_kernel(other_ref, pot_ref, log_ref, out_ref):
    line = halves(swap_halves(pot_ref[...] * SCALE))[1]
    for n in range(other_ref.shape[0] // LANES):
        logs = log_sum(jnp.stack([log_ref[n : n + 1, :], row_log_sums([other_ref[chunk(n), :] + line])]))
        out_ref[:, n : n + 1, :] = jnp.broadcast_to(logs[None], (out_ref.shape[0], 1, LANES))


def swap_halves(chunks):
    half = chunks.shape[0] // 2
    swapped = jnp.concatenate([chunks[half:], chunks[:half]], axis=0)
    return jnp.where(lax.axis_index("row") % 2 == 1, swapped, chunks)


def col_kernel(log_data, own_ref, other_ref, got_ref, out_ref, pot_ref):
    gen_rows, half = own_ref.shape
    row_pot = log_data - log_sum(got_ref[...])
    for n in range(gen_rows // LANES):
        pot_ref[chunk(n), :] = lanes_to_rows(row_pot[n : n + 1, :])
    lines = []
    for ref in (own_ref, other_ref):

        def tile(n):
            return ref[chunk(n), :] + jnp.concatenate([pot_ref[chunk(n), :]] * (half // LANES), axis=1)

        def folded(values):
            return values.reshape(LANES // 8, 8, half)

        top = jnp.full((8, half), -jnp.inf, jnp.float32)
        for n in range(gen_rows // LANES):
            top = jnp.maximum(top, jnp.max(folded(tile(n)), axis=0))
        top = jnp.max(top, axis=0, keepdims=True)
        total = jnp.zeros((8, half), jnp.float32)
        for n in range(gen_rows // LANES):
            total = total + jnp.sum(folded(jnp.exp2(tile(n) - top)), axis=0)
        lines.append(line_to_chunks(top + jnp.log2(jnp.sum(total, axis=0, keepdims=True))))
    chunks = swap_halves(jnp.concatenate(lines, axis=0))
    out_ref[...] = jnp.broadcast_to(chunks[None], out_ref.shape)


def row_kernel(log_gen, own_ref, other_ref, got_ref, out_ref):
    lines = halves(swap_halves(log_gen - log_sum(got_ref[...])))
    for n in range(own_ref.shape[0] // LANES):
        logs = row_log_sums([ref[chunk(n), :] + line for ref, line in zip((own_ref, other_ref), lines)])
        out_ref[:, n : n + 1, :] = jnp.broadcast_to(logs[None], (out_ref.shape[0], 1, LANES))


def merged(refs):
    stats = jnp.stack([ref[ref.shape[0] - STATS :, :] for ref in refs])
    tops, totals = stats[:, : STATS // 2, :], stats[:, STATS // 2 :, :]
    top = jnp.max(tops, axis=0)
    factors = jnp.exp2(tops - top[None])
    return top, jnp.sum(factors * totals, axis=0), factors


def add_blocks(offsets, data_refs, pieces, rows, out_refs):
    side = len(OFFSETS)
    feats = data_refs[0].shape[0] // side**2
    half = data_refs[0].shape[1]
    column, core = lax.axis_index("col"), lax.axis_index("row") % 2
    sources = []
    for offset in offsets:
        for second in range(side):
            y = jnp.where(core == 0, second, (column // side + offset + side) % side)
            x = jnp.where(core == 0, (column % side + offset + side) % side, second)
            sources.append(pl.ds(pl.multiple_of((y * side + x) * feats, feats), feats))
    dims = (((1,), (1,)), ((), ()))
    sums = 0.0
    for part, ref in enumerate(data_refs):
        data = jnp.concatenate([ref[source, :] for source in sources], axis=0)
        cols = slice(part * half, (part + 1) * half)
        for piece in pieces:
            sums = sums + lax.dot_general(data, piece[rows, cols], dims, preferred_element_type=jnp.float32)
    chunks = pieces[0].shape[0] // LANES
    for place in range(len(sources)):
        out_ref, second = out_refs[place // side], place % side
        for n in range(rows.start // LANES, rows.stop // LANES):
            lines = sums[place * feats : (place + 1) * feats, n * LANES - rows.start : (n + 1) * LANES - rows.start]
            start = (second * chunks + n) * feats
            out_ref[start : start + feats, :] = lines


GROUP = 2 * LANES


def target_kernel(log_gen, own_ref, other_ref, got_ref, data_ref, more_ref, pot_ref, *refs):
    *outs, stats_ref, high, low = refs
    gen_rows, half = own_ref.shape
    chunks = gen_rows // LANES
    pot = log_gen - log_sum(got_ref[...])
    pot_ref[...] = pot * (1.0 / SCALE)
    lines = halves(swap_halves(pot))
    for first in range(0, gen_rows, GROUP):
        for n in range(first // LANES, (first + GROUP) // LANES):
            tiles = [ref[chunk(n), :] + line for ref, line in zip((own_ref, other_ref), lines)]
            top = jnp.max(jnp.maximum(*tiles), axis=1, keepdims=True)
            total = 0.0
            for part, tile in enumerate(tiles):
                weights = jnp.exp2(tile - top)
                total = total + weights
                upper = weights.astype(jnp.bfloat16)
                cols = slice(part * half, (part + 1) * half)
                high[chunk(n), cols] = upper
                low[chunk(n), cols] = (weights - upper.astype(jnp.float32)).astype(jnp.bfloat16)
            total = jnp.sum(total, axis=1, keepdims=True)
            for place, column in ((n, top), (chunks + n, total)):
                stats_ref[place : place + 1, :] = rows_to_lanes(column)
        add_blocks(OFFSETS, (data_ref, more_ref), (high, low), slice(first, first + GROUP), outs)
    for out_ref in outs:
        out_ref[out_ref.shape[0] - STATS :, :] = stats_ref[...]


def relay_kernel(*refs):
    side = len(refs) // 2
    got, outs = refs[:side], refs[side:]
    top, total, factors = merged(got)
    chunks = top.shape[0]
    size = outs[0].shape[0] - STATS
    feats = size // chunks
    column, core = lax.axis_index("col"), lax.axis_index("row") % 2
    place = jnp.where(core == 0, column // side, column % side)
    for offset, out_ref in zip(OFFSETS, outs):
        start = (place + offset + side) % side * size
        for n in range(chunks):
            source = pl.ds(pl.multiple_of(start + n * feats, feats), feats)
            out_ref[n * feats : (n + 1) * feats, :] = sum(
                ref[source, :] * factors[sender, n : n + 1, :] for sender, ref in enumerate(got)
            )
        out_ref[size : size + chunks, :] = top
        out_ref[size + chunks :, :] = total


def merge_kernel(log_data, *refs):
    *got, gen_pot_ref, target_ref = refs
    top, total, factors = merged(got)
    feats = target_ref.shape[0]
    gen_pot_ref[...] = (log_data - (top + jnp.log2(total))) * (1.0 / SCALE)
    factors = factors / total[None]
    for n in range(top.shape[0]):
        target_ref[:, chunk(n)] = sum(
            ref[n * feats : (n + 1) * feats, :] * factors[sender, n : n + 1, :] for sender, ref in enumerate(got)
        )


def local(gen_points, data_points, data_potential):
    f32 = jnp.float32
    rows_n, cols_n = lax.axis_size("row"), lax.axis_size("col")
    gen_rows = gen_points.shape[0] * cols_n
    data_cols = data_points.shape[0]
    features = gen_points.shape[1]
    log_data = math.log2(data_cols * cols_n)
    log_gen = math.log2(gen_rows * rows_n)
    half = data_cols // 2
    gen_chunks, data_chunks = gen_rows // LANES, data_cols // LANES
    feats = features // cols_n
    dtype = gen_points.dtype
    shaped = jax.ShapeDtypeStruct

    side = math.isqrt(cols_n)

    def hop(array, phase, back):
        pairs = []
        for row in range(rows_n):
            for y in range(side):
                for x in range(side):
                    along_y = (row + phase) % 2
                    to_y, to_x = (y + back * along_y) % side, (x + back * (1 - along_y)) % side
                    pairs.append(((row * side + y) * side + x, (row * side + to_y) * side + to_x))
        return lax.ppermute(array, ("row", "col"), pairs)

    feats_held = data_points.shape[1]
    outgoing = kernel_call(
        layout_kernel,
        shaped((rows_n, feats_held, half), dtype),
        (pltpu.with_memory_space_constraint(data_points.T, pltpu.HBM),),
        scratch=[pltpu.VMEM((2, feats_held, half), dtype), pltpu.SemaphoreType.DMA((2 + rows_n,))],
        space=pltpu.HBM,
    )
    own = lax.all_to_all(outgoing, "row", 0, 0).reshape(features, half)
    stack = kernel_call(stack_kernel, shaped((side,) + gen_points.shape, dtype), (gen_points, *(hop(gen_points, 0, back) for back in OFFSETS[1:])))
    stacks = (stack,) + tuple(hop(stack, 1, back) for back in OFFSETS[1:])

    start = data_potential.reshape(data_chunks, LANES)

    own = kernel_call(ordered_kernel, pltpu.VMEM(own.shape, dtype), (own, *stacks[1:]), aliases={0: 0})
    other = in_vmem(lax.ppermute(own, "row", [(i, i ^ 1) for i in range(rows_n)]))
    own = in_vmem(own)
    row_out = pltpu.VMEM((cols_n, gen_chunks, LANES), f32)
    col_out = pltpu.VMEM((rows_n, data_chunks, LANES), f32)
    block = pltpu.VMEM((gen_rows, half), f32)

    def at(body, number):
        return lambda *refs: body(number, *refs)

    gen, own_affinity, logs = kernel_call(
        own_kernel,
        (pltpu.VMEM((gen_rows, features), dtype), block, pltpu.VMEM((gen_chunks, LANES), f32)),
        (*stacks, own, start),
        flops=2 * gen_rows * half * features,
    )
    affinity = (in_vmem(own_affinity), in_vmem(kernel_call(other_kernel, block, (gen, other))))
    lines = kernel_call(first_kernel, row_out, (affinity[1], start, in_vmem(logs)))
    for step in range(ITERS):
        got = lax.all_to_all(lines, "col", 0, 0)
        lines = kernel_call(
            at(col_kernel, log_data),
            col_out,
            (*affinity, got),
            scratch=[pltpu.VMEM((gen_rows, LANES), f32)],
        )
        got = lax.all_to_all(lines, "row", 0, 0)
        if step < ITERS - 1:
            lines = kernel_call(at(row_kernel, log_gen), row_out, (*affinity, got))
    block_rows = gen_chunks * feats
    sent = pltpu.VMEM((side * block_rows + STATS, LANES), f32)
    potential, *blocks = kernel_call(
        at(target_kernel, log_gen),
        (pltpu.VMEM((data_chunks, LANES), f32),) + (sent,) * side,
        (*affinity, got, own, other),
        scratch=[pltpu.VMEM((STATS, LANES), f32)] + [pltpu.VMEM((gen_rows, data_cols), dtype)] * 2,
    )
    blocks = kernel_call(
        relay_kernel,
        (shaped((block_rows + STATS, LANES), f32),) * side,
        [blocks[0]] + [hop(block, 0, back) for block, back in zip(blocks[1:], OFFSETS[1:])],
    )
    gen_pot, target = kernel_call(
        at(merge_kernel, log_data),
        (shaped((gen_chunks, LANES), f32), shaped((feats, gen_rows), f32)),
        [blocks[0]] + [hop(block, 1, back) for block, back in zip(blocks[1:], OFFSETS[1:])],
    )
    return (gen_pot.reshape(gen_rows), potential.reshape(data_cols), target)


def solution(mesh):
    placed = (P(("row", "col"), None), P("col", "row"), P("col"))
    return jax.shard_map(
        local,
        mesh=mesh,
        in_specs=placed,
        out_specs=(P("row"), P("col"), P("col", "row")),
        check_vma=False,
    )
```

```python
import functools
import math

import jax
import jax.numpy as jnp
from jax import lax
from jax.experimental import pallas as pl
from jax.experimental.pallas import tpu as pltpu
from jax.sharding import PartitionSpec as P

ITERS = 2
EPS = 0.05
LN2 = math.log(2.0)
SCALE = 1.0 / (EPS * LN2)
LANES = 128
OFFSETS = (0, 2, 1, -1)
GATHER = ((0, 1, 2, -1), (0, 1, 2, -1))
STATS = 8


def in_vmem(array):
    return pltpu.with_memory_space_constraint(array, pltpu.VMEM)


def kernel_call(body, out_shape, args, scratch=(), flops=None, aliases=(), space=pltpu.VMEM):
    whole = pl.BlockSpec(memory_space=space)
    return pl.pallas_call(
        body,
        out_shape=out_shape,
        in_specs=[whole] * len(args),
        out_specs=jax.tree.map(lambda _: whole, out_shape),
        scratch_shapes=list(scratch),
        input_output_aliases=dict(aliases),
        cost_estimate=flops and pl.CostEstimate(flops=flops, bytes_accessed=0, transcendentals=0),
        compiler_params=pltpu.CompilerParams(vmem_limit_bytes=16 * 1024 * 1024),
    )(*args)


def log_sum(parts):
    top = jnp.max(parts, axis=0)
    return top + jnp.log2(jnp.sum(jnp.exp2(parts - top[None]), axis=0))


def lanes_to_rows(chunk):
    return jnp.broadcast_to(chunk, (LANES, LANES)).T


def rows_to_lanes(column):
    return jnp.broadcast_to(column, (LANES, LANES)).T[0:1, :]


def chunks_to_line(chunks):
    return jnp.concatenate([chunks[n : n + 1, :] for n in range(chunks.shape[0])], axis=1)


def line_to_chunks(line):
    return jnp.concatenate([line[:, n : n + LANES] for n in range(0, line.shape[1], LANES)], axis=0)


def chunk(n):
    return slice(n * LANES, (n + 1) * LANES)


def halves(chunks):
    half = chunks.shape[0] // 2
    return [chunks_to_line(chunks[:half]), chunks_to_line(chunks[half:])]


def row_log_sums(tiles):
    top = jnp.max(functools.reduce(jnp.maximum, tiles), axis=1, keepdims=True)
    total = jnp.sum(sum(jnp.exp2(tile - top) for tile in tiles), axis=1, keepdims=True)
    return rows_to_lanes(top + jnp.log2(total))


def layout_kernel(data_ref, out_ref, held, sems):
    half = out_ref.shape[2]
    arrivals = [
        pltpu.make_async_copy(data_ref.at[:, pl.ds(part * half, half)], held.at[part], sems.at[part]) for part in range(2)
    ]
    copies = [pltpu.make_async_copy(held.at[n % 2], out_ref.at[n], sems.at[2 + n]) for n in range(out_ref.shape[0])]
    for arrival in arrivals:
        arrival.start()
    for part, arrival in enumerate(arrivals):
        arrival.wait()
        for copy in copies[part::2]:
            copy.start()
    for copy in copies:
        copy.wait()


def stack_kernel(*refs):
    for n, ref in enumerate(refs[:-1]):
        refs[-1][n, :, :] = ref[...]


def ordered_kernel(*_):
    pass


def affinity_chunks(gen_ref, data_ref):
    data = data_ref[...]
    data_f32 = data.astype(jnp.float32)
    data_sq = jnp.sum(data_f32 * data_f32, axis=0, keepdims=True)
    for n in range(gen_ref.shape[0] // LANES):
        gen = gen_ref[chunk(n), :]
        gen_f32 = gen.astype(jnp.float32)
        gen_sq = jnp.sum(gen_f32 * gen_f32, axis=1, keepdims=True)
        cross = jnp.dot(gen, data, preferred_element_type=jnp.float32)
        yield chunk(n), (2.0 * cross - (gen_sq + data_sq)) * (SCALE / gen.shape[1])


def own_kernel(g0, g1, g2, g3, data_ref, pot_ref, gen_ref, affinity_ref, log_ref):
    side, size = g0.shape[:2]
    column, core = lax.axis_index("col"), lax.axis_index("row") % 2
    for second, ref in zip(GATHER[1], (g0, g1, g2, g3)):
        for n, first in enumerate(GATHER[0]):
            y_back = jnp.where(core == 0, second, first)
            x_back = jnp.where(core == 0, first, second)
            place = (column // side - y_back + side) % side * side + (column % side - x_back + side) % side
            gen_ref[pl.ds(pl.multiple_of(place * size, size), size), :] = ref[n, :, :]
    line = halves(swap_halves(pot_ref[...] * SCALE))[0]
    for n, (rows, tile) in enumerate(affinity_chunks(gen_ref, data_ref)):
        affinity_ref[rows, :] = tile
        log_ref[n : n + 1, :] = row_log_sums([tile + line])


def other_kernel(gen_ref, data_ref, affinity_ref):
    for rows, tile in affinity_chunks(gen_ref, data_ref):
        affinity_ref[rows, :] = tile


def first_kernel(other_ref, pot_ref, log_ref, out_ref):
    line = halves(swap_halves(pot_ref[...] * SCALE))[1]
    for n in range(other_ref.shape[0] // LANES):
        logs = log_sum(jnp.stack([log_ref[n : n + 1, :], row_log_sums([other_ref[chunk(n), :] + line])]))
        out_ref[:, n : n + 1, :] = jnp.broadcast_to(logs[None], (out_ref.shape[0], 1, LANES))


def swap_halves(chunks):
    half = chunks.shape[0] // 2
    swapped = jnp.concatenate([chunks[half:], chunks[:half]], axis=0)
    return jnp.where(lax.axis_index("row") % 2 == 1, swapped, chunks)


def col_kernel(log_data, own_ref, other_ref, got_ref, out_ref, pot_ref):
    gen_rows, half = own_ref.shape
    row_pot = log_data - log_sum(got_ref[...])
    for n in range(gen_rows // LANES):
        pot_ref[chunk(n), :] = lanes_to_rows(row_pot[n : n + 1, :])
    lines = []
    for ref in (own_ref, other_ref):

        def tile(n):
            return ref[chunk(n), :] + jnp.concatenate([pot_ref[chunk(n), :]] * (half // LANES), axis=1)

        def folded(values):
            return values.reshape(LANES // 8, 8, half)

        top = jnp.full((8, half), -jnp.inf, jnp.float32)
        for n in range(gen_rows // LANES):
            top = jnp.maximum(top, jnp.max(folded(tile(n)), axis=0))
        top = jnp.max(top, axis=0, keepdims=True)
        total = jnp.zeros((8, half), jnp.float32)
        for n in range(gen_rows // LANES):
            total = total + jnp.sum(folded(jnp.exp2(tile(n) - top)), axis=0)
        lines.append(line_to_chunks(top + jnp.log2(jnp.sum(total, axis=0, keepdims=True))))
    chunks = swap_halves(jnp.concatenate(lines, axis=0))
    out_ref[...] = jnp.broadcast_to(chunks[None], out_ref.shape)


def row_kernel(log_gen, own_ref, other_ref, got_ref, out_ref):
    lines = halves(swap_halves(log_gen - log_sum(got_ref[...])))
    for n in range(own_ref.shape[0] // LANES):
        logs = row_log_sums([ref[chunk(n), :] + line for ref, line in zip((own_ref, other_ref), lines)])
        out_ref[:, n : n + 1, :] = jnp.broadcast_to(logs[None], (out_ref.shape[0], 1, LANES))


def merged(refs):
    stats = jnp.stack([ref[ref.shape[0] - STATS :, :] for ref in refs])
    tops, totals = stats[:, : STATS // 2, :], stats[:, STATS // 2 :, :]
    top = jnp.max(tops, axis=0)
    factors = jnp.exp2(tops - top[None])
    return top, jnp.sum(factors * totals, axis=0), factors


def add_blocks(offsets, data_refs, pieces, rows, out_refs):
    side = len(OFFSETS)
    feats = data_refs[0].shape[0] // side**2
    half = data_refs[0].shape[1]
    column, core = lax.axis_index("col"), lax.axis_index("row") % 2
    sources = []
    for offset in offsets:
        for second in range(side):
            y = jnp.where(core == 0, second, (column // side + offset + side) % side)
            x = jnp.where(core == 0, (column % side + offset + side) % side, second)
            sources.append(pl.ds(pl.multiple_of((y * side + x) * feats, feats), feats))
    dims = (((1,), (1,)), ((), ()))
    sums = 0.0
    for part, ref in enumerate(data_refs):
        data = jnp.concatenate([ref[source, :] for source in sources], axis=0)
        cols = slice(part * half, (part + 1) * half)
        for piece in pieces:
            sums = sums + lax.dot_general(data, piece[rows, cols], dims, preferred_element_type=jnp.float32)
    chunks = pieces[0].shape[0] // LANES
    for place in range(len(sources)):
        out_ref, second = out_refs[place // side], place % side
        for n in range(rows.start // LANES, rows.stop // LANES):
            lines = sums[place * feats : (place + 1) * feats, n * LANES - rows.start : (n + 1) * LANES - rows.start]
            start = (second * chunks + n) * feats
            out_ref[start : start + feats, :] = lines


GROUP = 2 * LANES


def target_kernel(log_gen, own_ref, other_ref, got_ref, data_ref, more_ref, pot_ref, *refs):
    stats_ref, high, low, *outs = refs
    gen_rows, half = own_ref.shape
    chunks = gen_rows // LANES
    pot = log_gen - log_sum(got_ref[...])
    pot_ref[...] = pot * (1.0 / SCALE)
    lines = halves(swap_halves(pot))
    for first in range(0, gen_rows, GROUP):
        for n in range(first // LANES, (first + GROUP) // LANES):
            tiles = [ref[chunk(n), :] + line for ref, line in zip((own_ref, other_ref), lines)]
            top = jnp.max(jnp.maximum(*tiles), axis=1, keepdims=True)
            total = 0.0
            for part, tile in enumerate(tiles):
                weights = jnp.exp2(tile - top)
                total = total + weights
                upper = weights.astype(jnp.bfloat16)
                cols = slice(part * half, (part + 1) * half)
                high[chunk(n), cols] = upper
                low[chunk(n), cols] = (weights - upper.astype(jnp.float32)).astype(jnp.bfloat16)
            total = jnp.sum(total, axis=1, keepdims=True)
            for place, column in ((n, top), (chunks + n, total)):
                stats_ref[place : place + 1, :] = rows_to_lanes(column)
        add_blocks(OFFSETS[1:], (data_ref, more_ref), (high, low), slice(first, first + GROUP), outs)
    for out_ref in outs:
        out_ref[out_ref.shape[0] - STATS :, :] = stats_ref[...]


def near_kernel(stats_ref, high, low, data_ref, more_ref, out_ref):
    for first in range(0, high.shape[0], GROUP):
        add_blocks(OFFSETS[:1], (data_ref, more_ref), (high, low), slice(first, first + GROUP), (out_ref,))
    out_ref[out_ref.shape[0] - STATS :, :] = stats_ref[...]


def relay_kernel(*refs):
    side = len(refs) // 2
    got, outs = refs[:side], refs[side:]
    top, total, factors = merged(got)
    chunks = top.shape[0]
    size = outs[0].shape[0] - STATS
    feats = size // chunks
    column, core = lax.axis_index("col"), lax.axis_index("row") % 2
    place = jnp.where(core == 0, column // side, column % side)
    for offset, out_ref in zip(OFFSETS, outs):
        start = (place + offset + side) % side * size
        for n in range(chunks):
            source = pl.ds(pl.multiple_of(start + n * feats, feats), feats)
            out_ref[n * feats : (n + 1) * feats, :] = sum(
                ref[source, :] * factors[sender, n : n + 1, :] for sender, ref in enumerate(got)
            )
        out_ref[size : size + chunks, :] = top
        out_ref[size + chunks :, :] = total


def merge_kernel(log_data, *refs):
    *got, gen_pot_ref, target_ref = refs
    top, total, factors = merged(got)
    feats = target_ref.shape[0]
    gen_pot_ref[...] = (log_data - (top + jnp.log2(total))) * (1.0 / SCALE)
    factors = factors / total[None]
    for n in range(top.shape[0]):
        target_ref[:, chunk(n)] = sum(
            ref[n * feats : (n + 1) * feats, :] * factors[sender, n : n + 1, :] for sender, ref in enumerate(got)
        )


def local(gen_points, data_points, data_potential):
    f32 = jnp.float32
    rows_n, cols_n = lax.axis_size("row"), lax.axis_size("col")
    gen_rows = gen_points.shape[0] * cols_n
    data_cols = data_points.shape[0]
    features = gen_points.shape[1]
    log_data = math.log2(data_cols * cols_n)
    log_gen = math.log2(gen_rows * rows_n)
    half = data_cols // 2
    gen_chunks, data_chunks = gen_rows // LANES, data_cols // LANES
    feats = features // cols_n
    dtype = gen_points.dtype
    shaped = jax.ShapeDtypeStruct

    side = math.isqrt(cols_n)

    def hop(array, phase, back):
        pairs = []
        for row in range(rows_n):
            for y in range(side):
                for x in range(side):
                    along_y = (row + phase) % 2
                    to_y, to_x = (y + back * along_y) % side, (x + back * (1 - along_y)) % side
                    pairs.append(((row * side + y) * side + x, (row * side + to_y) * side + to_x))
        return lax.ppermute(array, ("row", "col"), pairs)

    feats_held = data_points.shape[1]
    outgoing = kernel_call(
        layout_kernel,
        shaped((rows_n, feats_held, half), dtype),
        (pltpu.with_memory_space_constraint(data_points.T, pltpu.HBM),),
        scratch=[pltpu.VMEM((2, feats_held, half), dtype), pltpu.SemaphoreType.DMA((2 + rows_n,))],
        space=pltpu.HBM,
    )
    own = lax.all_to_all(outgoing, "row", 0, 0).reshape(features, half)
    stack = kernel_call(stack_kernel, shaped((side,) + gen_points.shape, dtype), (gen_points, *(hop(gen_points, 0, back) for back in GATHER[0][1:])))
    stacks = (stack,) + tuple(hop(stack, 1, back) for back in GATHER[1][1:])

    start = data_potential.reshape(data_chunks, LANES)

    own = kernel_call(ordered_kernel, pltpu.VMEM(own.shape, dtype), (own, *stacks[1:]), aliases={0: 0})
    other = in_vmem(lax.ppermute(own, "row", [(i, i ^ 1) for i in range(rows_n)]))
    own = in_vmem(own)
    row_out = pltpu.VMEM((cols_n, gen_chunks, LANES), f32)
    col_out = pltpu.VMEM((rows_n, data_chunks, LANES), f32)
    block = pltpu.VMEM((gen_rows, half), f32)

    def at(body, number):
        return lambda *refs: body(number, *refs)

    gen, own_affinity, logs = kernel_call(
        own_kernel,
        (pltpu.VMEM((gen_rows, features), dtype), block, pltpu.VMEM((gen_chunks, LANES), f32)),
        (*stacks, own, start),
        flops=2 * gen_rows * half * features,
    )
    affinity = (in_vmem(own_affinity), in_vmem(kernel_call(other_kernel, block, (gen, other))))
    lines = kernel_call(first_kernel, row_out, (affinity[1], start, in_vmem(logs)))
    for step in range(ITERS):
        got = lax.all_to_all(lines, "col", 0, 0)
        lines = kernel_call(
            at(col_kernel, log_data),
            col_out,
            (*affinity, got),
            scratch=[pltpu.VMEM((gen_rows, LANES), f32)],
        )
        got = lax.all_to_all(lines, "row", 0, 0)
        if step < ITERS - 1:
            lines = kernel_call(at(row_kernel, log_gen), row_out, (*affinity, got))
    block_rows = gen_chunks * feats
    sent = pltpu.VMEM((side * block_rows + STATS, LANES), f32)
    weights = pltpu.VMEM((gen_rows, data_cols), dtype)
    potential, stats, high, low, *blocks = kernel_call(
        at(target_kernel, log_gen),
        (pltpu.VMEM((data_chunks, LANES), f32), pltpu.VMEM((STATS, LANES), f32), weights, weights) + (sent,) * (side - 1),
        (*affinity, got, own, other),
    )
    kept = kernel_call(near_kernel, sent, (in_vmem(stats), in_vmem(high), in_vmem(low), own, other), flops=10**9)
    blocks = kernel_call(
        relay_kernel,
        (shaped((block_rows + STATS, LANES), f32),) * side,
        [in_vmem(kept)] + [hop(block, 0, back) for block, back in zip(blocks, OFFSETS[1:])],
    )
    gen_pot, target = kernel_call(
        at(merge_kernel, log_data),
        (shaped((gen_chunks, LANES), f32), shaped((feats, gen_rows), f32)),
        [blocks[0]] + [hop(block, 1, back) for block, back in zip(blocks[1:], OFFSETS[1:])],
    )
    return (gen_pot.reshape(gen_rows), potential.reshape(data_cols), target)


def solution(mesh):
    placed = (P(("row", "col"), None), P("col", "row"), P("col"))
    return jax.shard_map(
        local,
        mesh=mesh,
        in_specs=placed,
        out_specs=(P("row"), P("col"), P("col", "row")),
        check_vma=False,
    )
```

```python
import functools
import math

import jax
import jax.numpy as jnp
from jax import lax
from jax.experimental import pallas as pl
from jax.experimental.pallas import tpu as pltpu
from jax.sharding import PartitionSpec as P

ITERS = 2
EPS = 0.05
LN2 = math.log(2.0)
SCALE = 1.0 / (EPS * LN2)
LANES = 128
OFFSETS = (0, 2, 1, -1)
GATHER = ((0, -1, 1, 2), (0, 1, -1, 2))
STATS = 8


def in_vmem(array):
    return pltpu.with_memory_space_constraint(array, pltpu.VMEM)


def kernel_call(body, out_shape, args, scratch=(), flops=None, aliases=(), space=pltpu.VMEM):
    whole = pl.BlockSpec(memory_space=space)
    return pl.pallas_call(
        body,
        out_shape=out_shape,
        in_specs=[whole] * len(args),
        out_specs=jax.tree.map(lambda _: whole, out_shape),
        scratch_shapes=list(scratch),
        input_output_aliases=dict(aliases),
        cost_estimate=flops and pl.CostEstimate(flops=flops, bytes_accessed=0, transcendentals=0),
        compiler_params=pltpu.CompilerParams(vmem_limit_bytes=16 * 1024 * 1024),
    )(*args)


def log_sum(parts):
    top = jnp.max(parts, axis=0)
    return top + jnp.log2(jnp.sum(jnp.exp2(parts - top[None]), axis=0))


def lanes_to_rows(chunk):
    return jnp.broadcast_to(chunk, (LANES, LANES)).T


def rows_to_lanes(column):
    return jnp.broadcast_to(column, (LANES, LANES)).T[0:1, :]


def chunks_to_line(chunks):
    return jnp.concatenate([chunks[n : n + 1, :] for n in range(chunks.shape[0])], axis=1)


def line_to_chunks(line):
    return jnp.concatenate([line[:, n : n + LANES] for n in range(0, line.shape[1], LANES)], axis=0)


def chunk(n):
    return slice(n * LANES, (n + 1) * LANES)


def halves(chunks):
    half = chunks.shape[0] // 2
    return [chunks_to_line(chunks[:half]), chunks_to_line(chunks[half:])]


def row_log_sums(tiles):
    top = jnp.max(functools.reduce(jnp.maximum, tiles), axis=1, keepdims=True)
    total = jnp.sum(sum(jnp.exp2(tile - top) for tile in tiles), axis=1, keepdims=True)
    return rows_to_lanes(top + jnp.log2(total))


def layout_kernel(data_ref, out_ref, held, sems):
    half = out_ref.shape[2]
    arrivals = [
        pltpu.make_async_copy(data_ref.at[:, pl.ds(part * half, half)], held.at[part], sems.at[part]) for part in range(2)
    ]
    copies = [pltpu.make_async_copy(held.at[n % 2], out_ref.at[n], sems.at[2 + n]) for n in range(out_ref.shape[0])]
    for arrival in arrivals:
        arrival.start()
    for part, arrival in enumerate(arrivals):
        arrival.wait()
        for copy in copies[part::2]:
            copy.start()
    for copy in copies:
        copy.wait()


def stack_kernel(*refs):
    for n, ref in enumerate(refs[:-1]):
        refs[-1][n, :, :] = ref[...]


def ordered_kernel(*_):
    pass


def affinity_chunks(gen_ref, data_ref):
    data = data_ref[...]
    data_f32 = data.astype(jnp.float32)
    data_sq = jnp.sum(data_f32 * data_f32, axis=0, keepdims=True)
    for n in range(gen_ref.shape[0] // LANES):
        gen = gen_ref[chunk(n), :]
        gen_f32 = gen.astype(jnp.float32)
        gen_sq = jnp.sum(gen_f32 * gen_f32, axis=1, keepdims=True)
        cross = jnp.dot(gen, data, preferred_element_type=jnp.float32)
        yield chunk(n), (2.0 * cross - (gen_sq + data_sq)) * (SCALE / gen.shape[1])


def own_kernel(g0, g1, g2, g3, data_ref, pot_ref, gen_ref, affinity_ref, log_ref):
    side, size = g0.shape[:2]
    column, core = lax.axis_index("col"), lax.axis_index("row") % 2
    for second, ref in zip(GATHER[1], (g0, g1, g2, g3)):
        for n, first in enumerate(GATHER[0]):
            y_back = jnp.where(core == 0, second, first)
            x_back = jnp.where(core == 0, first, second)
            place = (column // side - y_back + side) % side * side + (column % side - x_back + side) % side
            gen_ref[pl.ds(pl.multiple_of(place * size, size), size), :] = ref[n, :, :]
    line = halves(swap_halves(pot_ref[...] * SCALE))[0]
    for n, (rows, tile) in enumerate(affinity_chunks(gen_ref, data_ref)):
        affinity_ref[rows, :] = tile
        log_ref[n : n + 1, :] = row_log_sums([tile + line])


def other_kernel(gen_ref, data_ref, affinity_ref):
    for rows, tile in affinity_chunks(gen_ref, data_ref):
        affinity_ref[rows, :] = tile


def first_kernel(other_ref, pot_ref, log_ref, out_ref):
    line = halves(swap_halves(pot_ref[...] * SCALE))[1]
    for n in range(other_ref.shape[0] // LANES):
        logs = log_sum(jnp.stack([log_ref[n : n + 1, :], row_log_sums([other_ref[chunk(n), :] + line])]))
        out_ref[:, n : n + 1, :] = jnp.broadcast_to(logs[None], (out_ref.shape[0], 1, LANES))


def swap_halves(chunks):
    half = chunks.shape[0] // 2
    swapped = jnp.concatenate([chunks[half:], chunks[:half]], axis=0)
    return jnp.where(lax.axis_index("row") % 2 == 1, swapped, chunks)


def col_kernel(log_data, own_ref, other_ref, got_ref, out_ref, pot_ref):
    gen_rows, half = own_ref.shape
    row_pot = log_data - log_sum(got_ref[...])
    for n in range(gen_rows // LANES):
        pot_ref[chunk(n), :] = lanes_to_rows(row_pot[n : n + 1, :])
    lines = []
    for ref in (own_ref, other_ref):

        def tile(n):
            return ref[chunk(n), :] + jnp.concatenate([pot_ref[chunk(n), :]] * (half // LANES), axis=1)

        def folded(values):
            return values.reshape(LANES // 8, 8, half)

        top = jnp.full((8, half), -jnp.inf, jnp.float32)
        for n in range(gen_rows // LANES):
            top = jnp.maximum(top, jnp.max(folded(tile(n)), axis=0))
        top = jnp.max(top, axis=0, keepdims=True)
        total = jnp.zeros((8, half), jnp.float32)
        for n in range(gen_rows // LANES):
            total = total + jnp.sum(folded(jnp.exp2(tile(n) - top)), axis=0)
        lines.append(line_to_chunks(top + jnp.log2(jnp.sum(total, axis=0, keepdims=True))))
    chunks = swap_halves(jnp.concatenate(lines, axis=0))
    out_ref[...] = jnp.broadcast_to(chunks[None], out_ref.shape)


def row_kernel(log_gen, own_ref, other_ref, got_ref, out_ref):
    lines = halves(swap_halves(log_gen - log_sum(got_ref[...])))
    for n in range(own_ref.shape[0] // LANES):
        logs = row_log_sums([ref[chunk(n), :] + line for ref, line in zip((own_ref, other_ref), lines)])
        out_ref[:, n : n + 1, :] = jnp.broadcast_to(logs[None], (out_ref.shape[0], 1, LANES))


def merged(refs):
    stats = jnp.stack([ref[ref.shape[0] - STATS :, :] for ref in refs])
    tops, totals = stats[:, : STATS // 2, :], stats[:, STATS // 2 :, :]
    top = jnp.max(tops, axis=0)
    factors = jnp.exp2(tops - top[None])
    return top, jnp.sum(factors * totals, axis=0), factors


def add_blocks(offsets, data_refs, pieces, rows, out_refs):
    side = len(OFFSETS)
    feats = data_refs[0].shape[0] // side**2
    half = data_refs[0].shape[1]
    column, core = lax.axis_index("col"), lax.axis_index("row") % 2
    sources = []
    for offset in offsets:
        for second in range(side):
            y = jnp.where(core == 0, second, (column // side + offset + side) % side)
            x = jnp.where(core == 0, (column % side + offset + side) % side, second)
            sources.append(pl.ds(pl.multiple_of((y * side + x) * feats, feats), feats))
    dims = (((1,), (1,)), ((), ()))
    sums = 0.0
    for part, ref in enumerate(data_refs):
        data = jnp.concatenate([ref[source, :] for source in sources], axis=0)
        cols = slice(part * half, (part + 1) * half)
        for piece in pieces:
            sums = sums + lax.dot_general(data, piece[rows, cols], dims, preferred_element_type=jnp.float32)
    chunks = pieces[0].shape[0] // LANES
    for place in range(len(sources)):
        out_ref, second = out_refs[place // side], place % side
        for n in range(rows.start // LANES, rows.stop // LANES):
            lines = sums[place * feats : (place + 1) * feats, n * LANES - rows.start : (n + 1) * LANES - rows.start]
            start = (second * chunks + n) * feats
            out_ref[start : start + feats, :] = lines


GROUP = 2 * LANES


def target_kernel(log_gen, own_ref, other_ref, got_ref, data_ref, more_ref, pot_ref, *refs):
    stats_ref, high, low, *outs = refs
    gen_rows, half = own_ref.shape
    chunks = gen_rows // LANES
    pot = log_gen - log_sum(got_ref[...])
    pot_ref[...] = pot * (1.0 / SCALE)
    lines = halves(swap_halves(pot))
    for first in range(0, gen_rows, GROUP):
        for n in range(first // LANES, (first + GROUP) // LANES):
            tiles = [ref[chunk(n), :] + line for ref, line in zip((own_ref, other_ref), lines)]
            top = jnp.max(jnp.maximum(*tiles), axis=1, keepdims=True)
            total = 0.0
            for part, tile in enumerate(tiles):
                weights = jnp.exp2(tile - top)
                total = total + weights
                upper = weights.astype(jnp.bfloat16)
                cols = slice(part * half, (part + 1) * half)
                high[chunk(n), cols] = upper
                low[chunk(n), cols] = (weights - upper.astype(jnp.float32)).astype(jnp.bfloat16)
            total = jnp.sum(total, axis=1, keepdims=True)
            for place, column in ((n, top), (chunks + n, total)):
                stats_ref[place : place + 1, :] = rows_to_lanes(column)
        add_blocks(OFFSETS[1:], (data_ref, more_ref), (high, low), slice(first, first + GROUP), outs)
    for out_ref in outs:
        out_ref[out_ref.shape[0] - STATS :, :] = stats_ref[...]


def near_kernel(stats_ref, high, low, data_ref, more_ref, out_ref):
    for first in range(0, high.shape[0], GROUP):
        add_blocks(OFFSETS[:1], (data_ref, more_ref), (high, low), slice(first, first + GROUP), (out_ref,))
    out_ref[out_ref.shape[0] - STATS :, :] = stats_ref[...]


def relay_kernel(*refs):
    side = len(refs) // 2
    got, outs = refs[:side], refs[side:]
    top, total, factors = merged(got)
    chunks = top.shape[0]
    size = outs[0].shape[0] - STATS
    feats = size // chunks
    column, core = lax.axis_index("col"), lax.axis_index("row") % 2
    place = jnp.where(core == 0, column // side, column % side)
    for offset, out_ref in zip(OFFSETS, outs):
        start = (place + offset + side) % side * size
        for n in range(chunks):
            source = pl.ds(pl.multiple_of(start + n * feats, feats), feats)
            out_ref[n * feats : (n + 1) * feats, :] = sum(
                ref[source, :] * factors[sender, n : n + 1, :] for sender, ref in enumerate(got)
            )
        out_ref[size : size + chunks, :] = top
        out_ref[size + chunks :, :] = total


def merge_kernel(log_data, *refs):
    *got, gen_pot_ref, target_ref = refs
    top, total, factors = merged(got)
    feats = target_ref.shape[0]
    gen_pot_ref[...] = (log_data - (top + jnp.log2(total))) * (1.0 / SCALE)
    factors = factors / total[None]
    for n in range(top.shape[0]):
        target_ref[:, chunk(n)] = sum(
            ref[n * feats : (n + 1) * feats, :] * factors[sender, n : n + 1, :] for sender, ref in enumerate(got)
        )


def local(gen_points, data_points, data_potential):
    f32 = jnp.float32
    rows_n, cols_n = lax.axis_size("row"), lax.axis_size("col")
    gen_rows = gen_points.shape[0] * cols_n
    data_cols = data_points.shape[0]
    features = gen_points.shape[1]
    log_data = math.log2(data_cols * cols_n)
    log_gen = math.log2(gen_rows * rows_n)
    half = data_cols // 2
    gen_chunks, data_chunks = gen_rows // LANES, data_cols // LANES
    feats = features // cols_n
    dtype = gen_points.dtype
    shaped = jax.ShapeDtypeStruct

    side = math.isqrt(cols_n)

    def hop(array, phase, back):
        pairs = []
        for row in range(rows_n):
            for y in range(side):
                for x in range(side):
                    along_y = (row + phase) % 2
                    to_y, to_x = (y + back * along_y) % side, (x + back * (1 - along_y)) % side
                    pairs.append(((row * side + y) * side + x, (row * side + to_y) * side + to_x))
        return lax.ppermute(array, ("row", "col"), pairs)

    feats_held = data_points.shape[1]
    outgoing = kernel_call(
        layout_kernel,
        shaped((rows_n, feats_held, half), dtype),
        (pltpu.with_memory_space_constraint(data_points.T, pltpu.HBM),),
        scratch=[pltpu.VMEM((2, feats_held, half), dtype), pltpu.SemaphoreType.DMA((2 + rows_n,))],
        space=pltpu.HBM,
    )
    own = lax.all_to_all(outgoing, "row", 0, 0).reshape(features, half)
    stack = kernel_call(stack_kernel, shaped((side,) + gen_points.shape, dtype), (gen_points, *(hop(gen_points, 0, back) for back in GATHER[0][1:])))
    stacks = (stack,) + tuple(hop(stack, 1, back) for back in GATHER[1][1:])

    start = data_potential.reshape(data_chunks, LANES)

    own = kernel_call(ordered_kernel, pltpu.VMEM(own.shape, dtype), (own, *stacks[1:]), aliases={0: 0})
    other = in_vmem(lax.ppermute(own, "row", [(i, i ^ 1) for i in range(rows_n)]))
    own = in_vmem(own)
    row_out = pltpu.VMEM((cols_n, gen_chunks, LANES), f32)
    col_out = pltpu.VMEM((rows_n, data_chunks, LANES), f32)
    block = pltpu.VMEM((gen_rows, half), f32)

    def at(body, number):
        return lambda *refs: body(number, *refs)

    gen, own_affinity, logs = kernel_call(
        own_kernel,
        (pltpu.VMEM((gen_rows, features), dtype), block, pltpu.VMEM((gen_chunks, LANES), f32)),
        (*stacks, own, start),
        flops=2 * gen_rows * half * features,
    )
    affinity = (in_vmem(own_affinity), in_vmem(kernel_call(other_kernel, block, (gen, other))))
    lines = kernel_call(first_kernel, row_out, (affinity[1], start, in_vmem(logs)))
    for step in range(ITERS):
        got = lax.all_to_all(lines, "col", 0, 0)
        lines = kernel_call(
            at(col_kernel, log_data),
            col_out,
            (*affinity, got),
            scratch=[pltpu.VMEM((gen_rows, LANES), f32)],
        )
        got = lax.all_to_all(lines, "row", 0, 0)
        if step < ITERS - 1:
            lines = kernel_call(at(row_kernel, log_gen), row_out, (*affinity, got))
    block_rows = gen_chunks * feats
    sent = pltpu.VMEM((side * block_rows + STATS, LANES), f32)
    weights = pltpu.VMEM((gen_rows, data_cols), dtype)
    potential, stats, high, low, *blocks = kernel_call(
        at(target_kernel, log_gen),
        (pltpu.VMEM((data_chunks, LANES), f32), pltpu.VMEM((STATS, LANES), f32), weights, weights) + (sent,) * (side - 1),
        (*affinity, got, own, other),
    )
    kept = kernel_call(near_kernel, sent, (in_vmem(stats), in_vmem(high), in_vmem(low), own, other), flops=10**9)
    blocks = kernel_call(
        relay_kernel,
        (shaped((block_rows + STATS, LANES), f32),) * side,
        [in_vmem(kept)] + [hop(block, 0, back) for block, back in zip(blocks, OFFSETS[1:])],
    )
    gen_pot, target = kernel_call(
        at(merge_kernel, log_data),
        (shaped((gen_chunks, LANES), f32), shaped((feats, gen_rows), f32)),
        [blocks[0]] + [hop(block, 1, back) for block, back in zip(blocks[1:], OFFSETS[1:])],
    )
    return (gen_pot.reshape(gen_rows), potential.reshape(data_cols), target)


def solution(mesh):
    placed = (P(("row", "col"), None), P("col", "row"), P("col"))
    return jax.shard_map(
        local,
        mesh=mesh,
        in_specs=placed,
        out_specs=(P("row"), P("col"), P("col", "row")),
        check_vma=False,
    )
```

```python
import functools
import math

import jax
import jax.numpy as jnp
from jax import lax
from jax.experimental import pallas as pl
from jax.experimental.pallas import tpu as pltpu
from jax.sharding import PartitionSpec as P

ITERS = 2
EPS = 0.05
LN2 = math.log(2.0)
SCALE = 1.0 / (EPS * LN2)
LANES = 128
OFFSETS = (0, 2, 1, -1)
GATHER = ((0, -1, 1, 2), (0, 1, -1, 2))
STATS = 8


def in_vmem(array):
    return pltpu.with_memory_space_constraint(array, pltpu.VMEM)


def kernel_call(body, out_shape, args, scratch=(), flops=None, aliases=(), space=pltpu.VMEM):
    whole = pl.BlockSpec(memory_space=space)
    return pl.pallas_call(
        body,
        out_shape=out_shape,
        in_specs=[whole] * len(args),
        out_specs=jax.tree.map(lambda _: whole, out_shape),
        scratch_shapes=list(scratch),
        input_output_aliases=dict(aliases),
        cost_estimate=flops and pl.CostEstimate(flops=flops, bytes_accessed=0, transcendentals=0),
        compiler_params=pltpu.CompilerParams(vmem_limit_bytes=16 * 1024 * 1024),
    )(*args)


def log_sum(parts):
    top = jnp.max(parts, axis=0)
    return top + jnp.log2(jnp.sum(jnp.exp2(parts - top[None]), axis=0))


def lanes_to_rows(chunk):
    return jnp.broadcast_to(chunk, (LANES, LANES)).T


def rows_to_lanes(column):
    return jnp.broadcast_to(column, (LANES, LANES)).T[0:1, :]


def chunks_to_line(chunks):
    return jnp.concatenate([chunks[n : n + 1, :] for n in range(chunks.shape[0])], axis=1)


def line_to_chunks(line):
    return jnp.concatenate([line[:, n : n + LANES] for n in range(0, line.shape[1], LANES)], axis=0)


def chunk(n):
    return slice(n * LANES, (n + 1) * LANES)


def halves(chunks):
    half = chunks.shape[0] // 2
    return [chunks_to_line(chunks[:half]), chunks_to_line(chunks[half:])]


def row_log_sums(tiles):
    top = jnp.max(functools.reduce(jnp.maximum, tiles), axis=1, keepdims=True)
    total = jnp.sum(sum(jnp.exp2(tile - top) for tile in tiles), axis=1, keepdims=True)
    return rows_to_lanes(top + jnp.log2(total))


def layout_kernel(data_ref, out_ref, held, sems):
    half = out_ref.shape[2]
    arrivals = [
        pltpu.make_async_copy(data_ref.at[:, pl.ds(part * half, half)], held.at[part], sems.at[part]) for part in range(2)
    ]
    copies = [pltpu.make_async_copy(held.at[n % 2], out_ref.at[n], sems.at[2 + n]) for n in range(out_ref.shape[0])]
    for arrival in arrivals:
        arrival.start()
    for part, arrival in enumerate(arrivals):
        arrival.wait()
        for copy in copies[part::2]:
            copy.start()
    for copy in copies:
        copy.wait()


def stack_kernel(*refs):
    for n, ref in enumerate(refs[:-1]):
        refs[-1][n, :, :] = ref[...]


def ordered_kernel(*_):
    pass


def affinity_chunks(gen_ref, data_ref):
    data = data_ref[...]
    data_f32 = data.astype(jnp.float32)
    data_sq = jnp.sum(data_f32 * data_f32, axis=0, keepdims=True)
    for n in range(gen_ref.shape[0] // LANES):
        gen = gen_ref[chunk(n), :]
        gen_f32 = gen.astype(jnp.float32)
        gen_sq = jnp.sum(gen_f32 * gen_f32, axis=1, keepdims=True)
        cross = jnp.dot(gen, data, preferred_element_type=jnp.float32)
        yield chunk(n), (2.0 * cross - (gen_sq + data_sq)) * (SCALE / gen.shape[1])


def own_kernel(g0, g1, g2, g3, data_ref, pot_ref, gen_ref, affinity_ref, log_ref):
    side, size = g0.shape[:2]
    column, core = lax.axis_index("col"), lax.axis_index("row") % 2
    for second, ref in zip(GATHER[1], (g0, g1, g2, g3)):
        for n, first in enumerate(GATHER[0]):
            y_back = jnp.where(core == 0, second, -first)
            x_back = jnp.where(core == 0, first, -second)
            place = (column // side - y_back + side) % side * side + (column % side - x_back + side) % side
            gen_ref[pl.ds(pl.multiple_of(place * size, size), size), :] = ref[n, :, :]
    line = halves(swap_halves(pot_ref[...] * SCALE))[0]
    for n, (rows, tile) in enumerate(affinity_chunks(gen_ref, data_ref)):
        affinity_ref[rows, :] = tile
        log_ref[n : n + 1, :] = row_log_sums([tile + line])


def other_kernel(gen_ref, data_ref, affinity_ref):
    for rows, tile in affinity_chunks(gen_ref, data_ref):
        affinity_ref[rows, :] = tile


def first_kernel(other_ref, pot_ref, log_ref, out_ref):
    line = halves(swap_halves(pot_ref[...] * SCALE))[1]
    for n in range(other_ref.shape[0] // LANES):
        logs = log_sum(jnp.stack([log_ref[n : n + 1, :], row_log_sums([other_ref[chunk(n), :] + line])]))
        out_ref[:, n : n + 1, :] = jnp.broadcast_to(logs[None], (out_ref.shape[0], 1, LANES))


def swap_halves(chunks):
    half = chunks.shape[0] // 2
    swapped = jnp.concatenate([chunks[half:], chunks[:half]], axis=0)
    return jnp.where(lax.axis_index("row") % 2 == 1, swapped, chunks)


def col_kernel(log_data, own_ref, other_ref, got_ref, out_ref, pot_ref):
    gen_rows, half = own_ref.shape
    row_pot = log_data - log_sum(got_ref[...])
    for n in range(gen_rows // LANES):
        pot_ref[chunk(n), :] = lanes_to_rows(row_pot[n : n + 1, :])
    lines = []
    for ref in (own_ref, other_ref):

        def tile(n):
            return ref[chunk(n), :] + jnp.concatenate([pot_ref[chunk(n), :]] * (half // LANES), axis=1)

        def folded(values):
            return values.reshape(LANES // 8, 8, half)

        top = jnp.full((8, half), -jnp.inf, jnp.float32)
        for n in range(gen_rows // LANES):
            top = jnp.maximum(top, jnp.max(folded(tile(n)), axis=0))
        top = jnp.max(top, axis=0, keepdims=True)
        total = jnp.zeros((8, half), jnp.float32)
        for n in range(gen_rows // LANES):
            total = total + jnp.sum(folded(jnp.exp2(tile(n) - top)), axis=0)
        lines.append(line_to_chunks(top + jnp.log2(jnp.sum(total, axis=0, keepdims=True))))
    chunks = swap_halves(jnp.concatenate(lines, axis=0))
    out_ref[...] = jnp.broadcast_to(chunks[None], out_ref.shape)


def row_kernel(log_gen, own_ref, other_ref, got_ref, out_ref):
    lines = halves(swap_halves(log_gen - log_sum(got_ref[...])))
    for n in range(own_ref.shape[0] // LANES):
        logs = row_log_sums([ref[chunk(n), :] + line for ref, line in zip((own_ref, other_ref), lines)])
        out_ref[:, n : n + 1, :] = jnp.broadcast_to(logs[None], (out_ref.shape[0], 1, LANES))


def merged(refs):
    stats = jnp.stack([ref[ref.shape[0] - STATS :, :] for ref in refs])
    tops, totals = stats[:, : STATS // 2, :], stats[:, STATS // 2 :, :]
    top = jnp.max(tops, axis=0)
    factors = jnp.exp2(tops - top[None])
    return top, jnp.sum(factors * totals, axis=0), factors


def add_blocks(offsets, data_refs, pieces, rows, out_refs):
    side = len(OFFSETS)
    feats = data_refs[0].shape[0] // side**2
    half = data_refs[0].shape[1]
    column, core = lax.axis_index("col"), lax.axis_index("row") % 2
    sources = []
    for offset in offsets:
        for second in range(side):
            y = jnp.where(core == 0, second, (column // side + offset + side) % side)
            x = jnp.where(core == 0, (column % side + offset + side) % side, second)
            sources.append(pl.ds(pl.multiple_of((y * side + x) * feats, feats), feats))
    dims = (((1,), (1,)), ((), ()))
    sums = 0.0
    for part, ref in enumerate(data_refs):
        data = jnp.concatenate([ref[source, :] for source in sources], axis=0)
        cols = slice(part * half, (part + 1) * half)
        for piece in pieces:
            sums = sums + lax.dot_general(data, piece[rows, cols], dims, preferred_element_type=jnp.float32)
    chunks = pieces[0].shape[0] // LANES
    for place in range(len(sources)):
        out_ref, second = out_refs[place // side], place % side
        for n in range(rows.start // LANES, rows.stop // LANES):
            lines = sums[place * feats : (place + 1) * feats, n * LANES - rows.start : (n + 1) * LANES - rows.start]
            start = (second * chunks + n) * feats
            out_ref[start : start + feats, :] = lines


GROUP = 2 * LANES


def target_kernel(log_gen, own_ref, other_ref, got_ref, data_ref, more_ref, pot_ref, *refs):
    stats_ref, high, low, *outs = refs
    gen_rows, half = own_ref.shape
    chunks = gen_rows // LANES
    pot = log_gen - log_sum(got_ref[...])
    pot_ref[...] = pot * (1.0 / SCALE)
    lines = halves(swap_halves(pot))
    for first in range(0, gen_rows, GROUP):
        for n in range(first // LANES, (first + GROUP) // LANES):
            tiles = [ref[chunk(n), :] + line for ref, line in zip((own_ref, other_ref), lines)]
            top = jnp.max(jnp.maximum(*tiles), axis=1, keepdims=True)
            total = 0.0
            for part, tile in enumerate(tiles):
                weights = jnp.exp2(tile - top)
                total = total + weights
                upper = weights.astype(jnp.bfloat16)
                cols = slice(part * half, (part + 1) * half)
                high[chunk(n), cols] = upper
                low[chunk(n), cols] = (weights - upper.astype(jnp.float32)).astype(jnp.bfloat16)
            total = jnp.sum(total, axis=1, keepdims=True)
            for place, column in ((n, top), (chunks + n, total)):
                stats_ref[place : place + 1, :] = rows_to_lanes(column)
        add_blocks(OFFSETS[1:], (data_ref, more_ref), (high, low), slice(first, first + GROUP), outs)
    for out_ref in outs:
        out_ref[out_ref.shape[0] - STATS :, :] = stats_ref[...]


def near_kernel(stats_ref, high, low, data_ref, more_ref, out_ref):
    for first in range(0, high.shape[0], GROUP):
        add_blocks(OFFSETS[:1], (data_ref, more_ref), (high, low), slice(first, first + GROUP), (out_ref,))
    out_ref[out_ref.shape[0] - STATS :, :] = stats_ref[...]


def relay_kernel(*refs):
    side = len(refs) // 2
    got, outs = refs[:side], refs[side:]
    top, total, factors = merged(got)
    chunks = top.shape[0]
    size = outs[0].shape[0] - STATS
    feats = size // chunks
    column, core = lax.axis_index("col"), lax.axis_index("row") % 2
    place = jnp.where(core == 0, column // side, column % side)
    for offset, out_ref in zip(OFFSETS, outs):
        start = (place + offset + side) % side * size
        for n in range(chunks):
            source = pl.ds(pl.multiple_of(start + n * feats, feats), feats)
            out_ref[n * feats : (n + 1) * feats, :] = sum(
                ref[source, :] * factors[sender, n : n + 1, :] for sender, ref in enumerate(got)
            )
        out_ref[size : size + chunks, :] = top
        out_ref[size + chunks :, :] = total


def merge_kernel(log_data, *refs):
    *got, gen_pot_ref, target_ref = refs
    top, total, factors = merged(got)
    feats = target_ref.shape[0]
    gen_pot_ref[...] = (log_data - (top + jnp.log2(total))) * (1.0 / SCALE)
    factors = factors / total[None]
    for n in range(top.shape[0]):
        target_ref[:, chunk(n)] = sum(
            ref[n * feats : (n + 1) * feats, :] * factors[sender, n : n + 1, :] for sender, ref in enumerate(got)
        )


def local(gen_points, data_points, data_potential):
    f32 = jnp.float32
    rows_n, cols_n = lax.axis_size("row"), lax.axis_size("col")
    gen_rows = gen_points.shape[0] * cols_n
    data_cols = data_points.shape[0]
    features = gen_points.shape[1]
    log_data = math.log2(data_cols * cols_n)
    log_gen = math.log2(gen_rows * rows_n)
    half = data_cols // 2
    gen_chunks, data_chunks = gen_rows // LANES, data_cols // LANES
    feats = features // cols_n
    dtype = gen_points.dtype
    shaped = jax.ShapeDtypeStruct

    side = math.isqrt(cols_n)

    def hop(array, phase, back, mirrored=False):
        pairs = []
        for row in range(rows_n):
            for y in range(side):
                for x in range(side):
                    along_y = (row + phase) % 2
                    way = -back if mirrored and row % 2 else back
                    to_y, to_x = (y + way * along_y) % side, (x + way * (1 - along_y)) % side
                    pairs.append(((row * side + y) * side + x, (row * side + to_y) * side + to_x))
        return lax.ppermute(array, ("row", "col"), pairs)

    feats_held = data_points.shape[1]
    outgoing = kernel_call(
        layout_kernel,
        shaped((rows_n, feats_held, half), dtype),
        (pltpu.with_memory_space_constraint(data_points.T, pltpu.HBM),),
        scratch=[pltpu.VMEM((2, feats_held, half), dtype), pltpu.SemaphoreType.DMA((2 + rows_n,))],
        space=pltpu.HBM,
    )
    own = lax.all_to_all(outgoing, "row", 0, 0).reshape(features, half)
    stack = kernel_call(stack_kernel, shaped((side,) + gen_points.shape, dtype), (gen_points, *(hop(gen_points, 0, back, True) for back in GATHER[0][1:])))
    stacks = (stack,) + tuple(hop(stack, 1, back, True) for back in GATHER[1][1:])

    start = data_potential.reshape(data_chunks, LANES)

    own = kernel_call(ordered_kernel, pltpu.VMEM(own.shape, dtype), (own, *stacks[1:]), aliases={0: 0})
    other = in_vmem(lax.ppermute(own, "row", [(i, i ^ 1) for i in range(rows_n)]))
    own = in_vmem(own)
    row_out = pltpu.VMEM((cols_n, gen_chunks, LANES), f32)
    col_out = pltpu.VMEM((rows_n, data_chunks, LANES), f32)
    block = pltpu.VMEM((gen_rows, half), f32)

    def at(body, number):
        return lambda *refs: body(number, *refs)

    gen, own_affinity, logs = kernel_call(
        own_kernel,
        (pltpu.VMEM((gen_rows, features), dtype), block, pltpu.VMEM((gen_chunks, LANES), f32)),
        (*stacks, own, start),
        flops=2 * gen_rows * half * features,
    )
    affinity = (in_vmem(own_affinity), in_vmem(kernel_call(other_kernel, block, (gen, other))))
    lines = kernel_call(first_kernel, row_out, (affinity[1], start, in_vmem(logs)))
    for step in range(ITERS):
        got = lax.all_to_all(lines, "col", 0, 0)
        lines = kernel_call(
            at(col_kernel, log_data),
            col_out,
            (*affinity, got),
            scratch=[pltpu.VMEM((gen_rows, LANES), f32)],
        )
        got = lax.all_to_all(lines, "row", 0, 0)
        if step < ITERS - 1:
            lines = kernel_call(at(row_kernel, log_gen), row_out, (*affinity, got))
    block_rows = gen_chunks * feats
    sent = pltpu.VMEM((side * block_rows + STATS, LANES), f32)
    weights = pltpu.VMEM((gen_rows, data_cols), dtype)
    potential, stats, high, low, *blocks = kernel_call(
        at(target_kernel, log_gen),
        (pltpu.VMEM((data_chunks, LANES), f32), pltpu.VMEM((STATS, LANES), f32), weights, weights) + (sent,) * (side - 1),
        (*affinity, got, own, other),
    )
    kept = kernel_call(near_kernel, sent, (in_vmem(stats), in_vmem(high), in_vmem(low), own, other), flops=10**9)
    blocks = kernel_call(
        relay_kernel,
        (shaped((block_rows + STATS, LANES), f32),) * side,
        [in_vmem(kept)] + [hop(block, 0, back) for block, back in zip(blocks, OFFSETS[1:])],
    )
    gen_pot, target = kernel_call(
        at(merge_kernel, log_data),
        (shaped((gen_chunks, LANES), f32), shaped((feats, gen_rows), f32)),
        [blocks[0]] + [hop(block, 1, back) for block, back in zip(blocks[1:], OFFSETS[1:])],
    )
    return (gen_pot.reshape(gen_rows), potential.reshape(data_cols), target)


def solution(mesh):
    placed = (P(("row", "col"), None), P("col", "row"), P("col"))
    return jax.shard_map(
        local,
        mesh=mesh,
        in_specs=placed,
        out_specs=(P("row"), P("col"), P("col", "row")),
        check_vma=False,
    )
```

```python
import functools
import math

import jax
import jax.numpy as jnp
from jax import lax
from jax.experimental import pallas as pl
from jax.experimental.pallas import tpu as pltpu
from jax.sharding import PartitionSpec as P

ITERS = 2
EPS = 0.05
LN2 = math.log(2.0)
SCALE = 1.0 / (EPS * LN2)
LANES = 128
OFFSETS = (0, 2, 1, -1)
RELAY = (0, 1, 2, -1)
GATHER = ((0, -1, 1, 2), (0, 1, -1, 2))
STATS = 8


def in_vmem(array):
    return pltpu.with_memory_space_constraint(array, pltpu.VMEM)


def kernel_call(body, out_shape, args, scratch=(), flops=None, aliases=(), space=pltpu.VMEM):
    whole = pl.BlockSpec(memory_space=space)
    return pl.pallas_call(
        body,
        out_shape=out_shape,
        in_specs=[whole] * len(args),
        out_specs=jax.tree.map(lambda _: whole, out_shape),
        scratch_shapes=list(scratch),
        input_output_aliases=dict(aliases),
        cost_estimate=flops and pl.CostEstimate(flops=flops, bytes_accessed=0, transcendentals=0),
        compiler_params=pltpu.CompilerParams(vmem_limit_bytes=16 * 1024 * 1024),
    )(*args)


def log_sum(parts):
    top = jnp.max(parts, axis=0)
    return top + jnp.log2(jnp.sum(jnp.exp2(parts - top[None]), axis=0))


def lanes_to_rows(chunk):
    return jnp.broadcast_to(chunk, (LANES, LANES)).T


def rows_to_lanes(column):
    return jnp.broadcast_to(column, (LANES, LANES)).T[0:1, :]


def chunks_to_line(chunks):
    return jnp.concatenate([chunks[n : n + 1, :] for n in range(chunks.shape[0])], axis=1)


def line_to_chunks(line):
    return jnp.concatenate([line[:, n : n + LANES] for n in range(0, line.shape[1], LANES)], axis=0)


def chunk(n):
    return slice(n * LANES, (n + 1) * LANES)


def halves(chunks):
    half = chunks.shape[0] // 2
    return [chunks_to_line(chunks[:half]), chunks_to_line(chunks[half:])]


def row_log_sums(tiles):
    top = jnp.max(functools.reduce(jnp.maximum, tiles), axis=1, keepdims=True)
    total = jnp.sum(sum(jnp.exp2(tile - top) for tile in tiles), axis=1, keepdims=True)
    return rows_to_lanes(top + jnp.log2(total))


def layout_kernel(data_ref, out_ref, held, sems):
    half = out_ref.shape[2]
    arrivals = [
        pltpu.make_async_copy(data_ref.at[:, pl.ds(part * half, half)], held.at[part], sems.at[part]) for part in range(2)
    ]
    copies = [pltpu.make_async_copy(held.at[n % 2], out_ref.at[n], sems.at[2 + n]) for n in range(out_ref.shape[0])]
    for arrival in arrivals:
        arrival.start()
    for part, arrival in enumerate(arrivals):
        arrival.wait()
        for copy in copies[part::2]:
            copy.start()
    for copy in copies:
        copy.wait()


def stack_kernel(*refs):
    for n, ref in enumerate(refs[:-1]):
        refs[-1][n, :, :] = ref[...]


def ordered_kernel(*_):
    pass


def affinity_chunks(gen_ref, data_ref):
    data = data_ref[...]
    data_f32 = data.astype(jnp.float32)
    data_sq = jnp.sum(data_f32 * data_f32, axis=0, keepdims=True)
    for n in range(gen_ref.shape[0] // LANES):
        gen = gen_ref[chunk(n), :]
        gen_f32 = gen.astype(jnp.float32)
        gen_sq = jnp.sum(gen_f32 * gen_f32, axis=1, keepdims=True)
        cross = jnp.dot(gen, data, preferred_element_type=jnp.float32)
        yield chunk(n), (2.0 * cross - (gen_sq + data_sq)) * (SCALE / gen.shape[1])


def own_kernel(g0, g1, g2, g3, data_ref, pot_ref, gen_ref, affinity_ref, log_ref):
    side, size = g0.shape[:2]
    column, core = lax.axis_index("col"), lax.axis_index("row") % 2
    for second, ref in zip(GATHER[1], (g0, g1, g2, g3)):
        for n, first in enumerate(GATHER[0]):
            y_back = jnp.where(core == 0, second, -first)
            x_back = jnp.where(core == 0, first, -second)
            place = (column // side - y_back + side) % side * side + (column % side - x_back + side) % side
            gen_ref[pl.ds(pl.multiple_of(place * size, size), size), :] = ref[n, :, :]
    line = halves(swap_halves(pot_ref[...] * SCALE))[0]
    for n, (rows, tile) in enumerate(affinity_chunks(gen_ref, data_ref)):
        affinity_ref[rows, :] = tile
        log_ref[n : n + 1, :] = row_log_sums([tile + line])


def other_kernel(gen_ref, data_ref, affinity_ref):
    for rows, tile in affinity_chunks(gen_ref, data_ref):
        affinity_ref[rows, :] = tile


def first_kernel(other_ref, pot_ref, log_ref, out_ref):
    line = halves(swap_halves(pot_ref[...] * SCALE))[1]
    for n in range(other_ref.shape[0] // LANES):
        logs = log_sum(jnp.stack([log_ref[n : n + 1, :], row_log_sums([other_ref[chunk(n), :] + line])]))
        out_ref[:, n : n + 1, :] = jnp.broadcast_to(logs[None], (out_ref.shape[0], 1, LANES))


def swap_halves(chunks):
    half = chunks.shape[0] // 2
    swapped = jnp.concatenate([chunks[half:], chunks[:half]], axis=0)
    return jnp.where(lax.axis_index("row") % 2 == 1, swapped, chunks)


def col_kernel(log_data, own_ref, other_ref, got_ref, out_ref, pot_ref):
    gen_rows, half = own_ref.shape
    row_pot = log_data - log_sum(got_ref[...])
    for n in range(gen_rows // LANES):
        pot_ref[chunk(n), :] = lanes_to_rows(row_pot[n : n + 1, :])
    lines = []
    for ref in (own_ref, other_ref):

        def tile(n):
            return ref[chunk(n), :] + jnp.concatenate([pot_ref[chunk(n), :]] * (half // LANES), axis=1)

        def folded(values):
            return values.reshape(LANES // 8, 8, half)

        top = jnp.full((8, half), -jnp.inf, jnp.float32)
        for n in range(gen_rows // LANES):
            top = jnp.maximum(top, jnp.max(folded(tile(n)), axis=0))
        top = jnp.max(top, axis=0, keepdims=True)
        total = jnp.zeros((8, half), jnp.float32)
        for n in range(gen_rows // LANES):
            total = total + jnp.sum(folded(jnp.exp2(tile(n) - top)), axis=0)
        lines.append(line_to_chunks(top + jnp.log2(jnp.sum(total, axis=0, keepdims=True))))
    chunks = swap_halves(jnp.concatenate(lines, axis=0))
    out_ref[...] = jnp.broadcast_to(chunks[None], out_ref.shape)


def row_kernel(log_gen, own_ref, other_ref, got_ref, out_ref):
    lines = halves(swap_halves(log_gen - log_sum(got_ref[...])))
    for n in range(own_ref.shape[0] // LANES):
        logs = row_log_sums([ref[chunk(n), :] + line for ref, line in zip((own_ref, other_ref), lines)])
        out_ref[:, n : n + 1, :] = jnp.broadcast_to(logs[None], (out_ref.shape[0], 1, LANES))


def merged(refs):
    stats = jnp.stack([ref[ref.shape[0] - STATS :, :] for ref in refs])
    tops, totals = stats[:, : STATS // 2, :], stats[:, STATS // 2 :, :]
    top = jnp.max(tops, axis=0)
    factors = jnp.exp2(tops - top[None])
    return top, jnp.sum(factors * totals, axis=0), factors


def add_blocks(offsets, data_refs, pieces, rows, out_refs):
    side = len(OFFSETS)
    feats = data_refs[0].shape[0] // side**2
    half = data_refs[0].shape[1]
    column, core = lax.axis_index("col"), lax.axis_index("row") % 2
    sources = []
    for offset in offsets:
        for second in range(side):
            y = jnp.where(core == 0, second, (column // side + offset + side) % side)
            x = jnp.where(core == 0, (column % side + offset + side) % side, second)
            sources.append(pl.ds(pl.multiple_of((y * side + x) * feats, feats), feats))
    dims = (((1,), (1,)), ((), ()))
    sums = 0.0
    for part, ref in enumerate(data_refs):
        data = jnp.concatenate([ref[source, :] for source in sources], axis=0)
        cols = slice(part * half, (part + 1) * half)
        for piece in pieces:
            sums = sums + lax.dot_general(data, piece[rows, cols], dims, preferred_element_type=jnp.float32)
    chunks = pieces[0].shape[0] // LANES
    for place in range(len(sources)):
        out_ref, second = out_refs[place // side], place % side
        for n in range(rows.start // LANES, rows.stop // LANES):
            lines = sums[place * feats : (place + 1) * feats, n * LANES - rows.start : (n + 1) * LANES - rows.start]
            start = (second * chunks + n) * feats
            out_ref[start : start + feats, :] = lines


GROUP = 2 * LANES


def target_kernel(log_gen, own_ref, other_ref, got_ref, data_ref, more_ref, pot_ref, *refs):
    stats_ref, high, low, *outs = refs
    gen_rows, half = own_ref.shape
    chunks = gen_rows // LANES
    pot = log_gen - log_sum(got_ref[...])
    pot_ref[...] = pot * (1.0 / SCALE)
    lines = halves(swap_halves(pot))
    for first in range(0, gen_rows, GROUP):
        for n in range(first // LANES, (first + GROUP) // LANES):
            tiles = [ref[chunk(n), :] + line for ref, line in zip((own_ref, other_ref), lines)]
            top = jnp.max(jnp.maximum(*tiles), axis=1, keepdims=True)
            total = 0.0
            for part, tile in enumerate(tiles):
                weights = jnp.exp2(tile - top)
                total = total + weights
                upper = weights.astype(jnp.bfloat16)
                cols = slice(part * half, (part + 1) * half)
                high[chunk(n), cols] = upper
                low[chunk(n), cols] = (weights - upper.astype(jnp.float32)).astype(jnp.bfloat16)
            total = jnp.sum(total, axis=1, keepdims=True)
            for place, column in ((n, top), (chunks + n, total)):
                stats_ref[place : place + 1, :] = rows_to_lanes(column)
        add_blocks(OFFSETS[1:], (data_ref, more_ref), (high, low), slice(first, first + GROUP), outs)
    for out_ref in outs:
        out_ref[out_ref.shape[0] - STATS :, :] = stats_ref[...]


def near_kernel(stats_ref, high, low, data_ref, more_ref, out_ref):
    for first in range(0, high.shape[0], GROUP):
        add_blocks(OFFSETS[:1], (data_ref, more_ref), (high, low), slice(first, first + GROUP), (out_ref,))
    out_ref[out_ref.shape[0] - STATS :, :] = stats_ref[...]


def relay_kernel(*refs):
    side = len(refs) // 2
    got, outs = refs[:side], refs[side:]
    top, total, factors = merged(got)
    chunks = top.shape[0]
    size = outs[0].shape[0] - STATS
    feats = size // chunks
    column, core = lax.axis_index("col"), lax.axis_index("row") % 2
    place = jnp.where(core == 0, column // side, column % side)
    for offset, out_ref in zip(RELAY, outs):
        start = (place + offset + side) % side * size
        for n in range(chunks):
            source = pl.ds(pl.multiple_of(start + n * feats, feats), feats)
            out_ref[n * feats : (n + 1) * feats, :] = sum(
                ref[source, :] * factors[sender, n : n + 1, :] for sender, ref in enumerate(got)
            )
        out_ref[size : size + chunks, :] = top
        out_ref[size + chunks :, :] = total


def merge_kernel(log_data, *refs):
    *got, gen_pot_ref, target_ref = refs
    top, total, factors = merged(got)
    feats = target_ref.shape[0]
    gen_pot_ref[...] = (log_data - (top + jnp.log2(total))) * (1.0 / SCALE)
    factors = factors / total[None]
    for n in range(top.shape[0]):
        target_ref[:, chunk(n)] = sum(
            ref[n * feats : (n + 1) * feats, :] * factors[sender, n : n + 1, :] for sender, ref in enumerate(got)
        )


def local(gen_points, data_points, data_potential):
    f32 = jnp.float32
    rows_n, cols_n = lax.axis_size("row"), lax.axis_size("col")
    gen_rows = gen_points.shape[0] * cols_n
    data_cols = data_points.shape[0]
    features = gen_points.shape[1]
    log_data = math.log2(data_cols * cols_n)
    log_gen = math.log2(gen_rows * rows_n)
    half = data_cols // 2
    gen_chunks, data_chunks = gen_rows // LANES, data_cols // LANES
    feats = features // cols_n
    dtype = gen_points.dtype
    shaped = jax.ShapeDtypeStruct

    side = math.isqrt(cols_n)

    def hop(array, phase, back, mirrored=False):
        pairs = []
        for row in range(rows_n):
            for y in range(side):
                for x in range(side):
                    along_y = (row + phase) % 2
                    way = -back if mirrored and row % 2 else back
                    to_y, to_x = (y + way * along_y) % side, (x + way * (1 - along_y)) % side
                    pairs.append(((row * side + y) * side + x, (row * side + to_y) * side + to_x))
        return lax.ppermute(array, ("row", "col"), pairs)

    feats_held = data_points.shape[1]
    outgoing = kernel_call(
        layout_kernel,
        shaped((rows_n, feats_held, half), dtype),
        (pltpu.with_memory_space_constraint(data_points.T, pltpu.HBM),),
        scratch=[pltpu.VMEM((2, feats_held, half), dtype), pltpu.SemaphoreType.DMA((2 + rows_n,))],
        space=pltpu.HBM,
    )
    own = lax.all_to_all(outgoing, "row", 0, 0).reshape(features, half)
    stack = kernel_call(stack_kernel, shaped((side,) + gen_points.shape, dtype), (gen_points, *(hop(gen_points, 0, back, True) for back in GATHER[0][1:])))
    stacks = (stack,) + tuple(hop(stack, 1, back, True) for back in GATHER[1][1:])

    start = data_potential.reshape(data_chunks, LANES)

    own = kernel_call(ordered_kernel, pltpu.VMEM(own.shape, dtype), (own, *stacks[1:]), aliases={0: 0})
    other = in_vmem(lax.ppermute(own, "row", [(i, i ^ 1) for i in range(rows_n)]))
    own = in_vmem(own)
    row_out = pltpu.VMEM((cols_n, gen_chunks, LANES), f32)
    col_out = pltpu.VMEM((rows_n, data_chunks, LANES), f32)
    block = pltpu.VMEM((gen_rows, half), f32)

    def at(body, number):
        return lambda *refs: body(number, *refs)

    gen, own_affinity, logs = kernel_call(
        own_kernel,
        (pltpu.VMEM((gen_rows, features), dtype), block, pltpu.VMEM((gen_chunks, LANES), f32)),
        (*stacks, own, start),
        flops=2 * gen_rows * half * features,
    )
    affinity = (in_vmem(own_affinity), in_vmem(kernel_call(other_kernel, block, (gen, other))))
    lines = kernel_call(first_kernel, row_out, (affinity[1], start, in_vmem(logs)))
    for step in range(ITERS):
        got = lax.all_to_all(lines, "col", 0, 0)
        lines = kernel_call(
            at(col_kernel, log_data),
            col_out,
            (*affinity, got),
            scratch=[pltpu.VMEM((gen_rows, LANES), f32)],
        )
        got = lax.all_to_all(lines, "row", 0, 0)
        if step < ITERS - 1:
            lines = kernel_call(at(row_kernel, log_gen), row_out, (*affinity, got))
    block_rows = gen_chunks * feats
    sent = pltpu.VMEM((side * block_rows + STATS, LANES), f32)
    weights = pltpu.VMEM((gen_rows, data_cols), dtype)
    potential, stats, high, low, *blocks = kernel_call(
        at(target_kernel, log_gen),
        (pltpu.VMEM((data_chunks, LANES), f32), pltpu.VMEM((STATS, LANES), f32), weights, weights) + (sent,) * (side - 1),
        (*affinity, got, own, other),
    )
    kept = kernel_call(near_kernel, sent, (in_vmem(stats), in_vmem(high), in_vmem(low), own, other), flops=10**9)
    blocks = kernel_call(
        relay_kernel,
        (shaped((block_rows + STATS, LANES), f32),) * side,
        [in_vmem(kept)] + [hop(block, 0, back) for block, back in zip(blocks, OFFSETS[1:])],
    )
    gen_pot, target = kernel_call(
        at(merge_kernel, log_data),
        (shaped((gen_chunks, LANES), f32), shaped((feats, gen_rows), f32)),
        [blocks[0]] + [hop(block, 1, back) for block, back in zip(blocks[1:], RELAY[1:])],
    )
    return (gen_pot.reshape(gen_rows), potential.reshape(data_cols), target)


def solution(mesh):
    placed = (P(("row", "col"), None), P("col", "row"), P("col"))
    return jax.shard_map(
        local,
        mesh=mesh,
        in_specs=placed,
        out_specs=(P("row"), P("col"), P("col", "row")),
        check_vma=False,
    )
```
